512 devices in a mesh: rows: 64 (over x, z, core), cols: 8 (over y).
Axes of the slice: x: 4, y: 8, z: 8, core: 2. Of those that a mesh axis runs over, the one named last changes fastest.
Arguments:
- momentum: float32 [3584, 13312], P('rows', 'cols'), may hold values from -200 to 200
Outputs:
- update: bfloat16 [3584, 13312], P('rows', 'cols')
The draws below stay inside these ranges and needn't reach their ends.
All inputs are finite; a program needn't handle non-finite values.
Results may differ from the reference program's by a relative error of at most 0.0052.
Values may be sent and summed in bfloat16 or wider, within the bound.
No kernel may reach another device: no remote copies, remote signals or barrier semaphores. Data moves between devices by JAX's collectives and lax.ppermute only.
A program may use at most 64 MiB of HBM per device.

```python
import math
import jax
import jax.numpy as jnp

M = 3584
N = 13312


def draw_momentum(key, part):
    key = jax.random.fold_in(key, 11)
    key_noise, key_rows, key_cols = jax.random.split(key, 3)
    row_pos = jnp.arange(M, dtype=jnp.float32) / float(M - 1)
    row_scale = jnp.exp(jax.random.uniform(key_rows, (M, 1), jnp.float32) * math.log(3.0)) * jnp.exp(row_pos[:, None] * math.log(3.0))
    col_scale = jnp.exp(jax.random.uniform(key_cols, (1, N), jnp.float32) * math.log(3.0))
    noise = jnp.clip(jax.random.normal(key_noise, (M, N), jnp.float32), -6.0, 6.0)
    return (noise * row_scale * col_scale).astype(jnp.float32)


def setup_inputs(seed: int = 0) -> dict:
    key_list = jax.random.split(jax.random.key(seed), 2)
    return {
        "momentum": draw_momentum(jax.random.fold_in(key_list[1], 71), 0),
    }


coef_a = 3.4445
coef_b = -4.775
coef_c = 2.0315

def reference(momentum):
    total = jnp.sum(momentum * momentum)
    factor = math.sqrt(M) / 3.0 / (jnp.sqrt(total) + 1e-07)
    iterate = (momentum * factor).astype(jnp.bfloat16)
    gram = jnp.dot(iterate, iterate.T, preferred_element_type=jnp.float32).astype(jnp.bfloat16)
    square = jnp.dot(gram, gram, preferred_element_type=jnp.float32).astype(jnp.bfloat16)
    polynomial = (coef_b * gram.astype(jnp.float32) + coef_c * square.astype(jnp.float32)).astype(jnp.bfloat16)
    product = jnp.dot(polynomial, iterate, preferred_element_type=jnp.float32)
    scaled = (coef_a * iterate.astype(jnp.float32) + product) * (0.2 * math.sqrt(N))
    return scaled.astype(jnp.bfloat16)
```

```python
import math

import jax
import jax.numpy as jnp
from jax import lax
from jax.sharding import Mesh, PartitionSpec as P

M = 3584
N = 13312

coef_a = 3.4445
coef_b = -4.775
coef_c = 2.0315

lift = 128.0

bf16 = jnp.bfloat16
f32 = jnp.float32


def shift(size, by):
    return [(i, (i + by) % size) for i in range(size)]


def swap(size, bit):
    return [(i, i ^ bit) for i in range(size)]


def ring_z(block, total, steps):
    up, down = [block], []
    left, right = block, block
    for step in range(4):
        left, right, total = lax.optimization_barrier((left, right, total))
        left = lax.ppermute(left, "z", shift(8, 1))
        if step < 3:
            right = lax.ppermute(right, "z", shift(8, -1))
            down.append(right)
        up.append(left)
        total = add_swapped(total, *steps[step])
    return jnp.concatenate(up + down, axis=0), total


def add_swapped(total, axis, size, bit):
    return total + lax.ppermute(total, axis, swap(size, bit))


def spread(partial_rows, core):
    mine = lax.dynamic_index_in_dim(partial_rows, core, 0, keepdims=False)
    other = lax.dynamic_index_in_dim(partial_rows, 1 - core, 0, keepdims=False)
    got = lax.ppermute(other.astype(bf16), "c", swap(2, 1))
    pieces = (mine + got.astype(f32)).astype(bf16)
    pieces = lax.all_to_all(pieces, "x", 0, 0)
    return jnp.sum(pieces.astype(f32), axis=0)


def per_device(momentum):
    core = lax.axis_index("c")
    raw = (momentum * lift).astype(bf16)
    total = jnp.broadcast_to(jnp.sum(momentum * momentum).reshape(1, 1), (8, 128))

    rows_j, total = ring_z(
        raw, total, (("c", 2, 1), ("z", 8, 1), ("z", 8, 2), ("z", 8, 4))
    )
    over_x = lax.all_to_all(jnp.broadcast_to(raw[None], (4, 56, 1664)), "x", 0, 0)
    other_x = lax.ppermute(over_x, "c", swap(2, 1))
    first = jnp.where(core == 0, over_x, other_x)
    second = jnp.where(core == 0, other_x, over_x)
    rows_r = jnp.concatenate([first, second], axis=0).reshape(448, 1664)

    part = lax.dot_general(
        rows_j, rows_r, (((1,), (1,)), ((), ())), preferred_element_type=f32
    ).astype(bf16)
    part = lax.all_to_all(part.reshape(8, 56, 448), "y", 0, 0)
    piece = jnp.sum(part.astype(f32), axis=0).astype(bf16)
    gram = lax.all_to_all(
        jnp.broadcast_to(piece[None], (8, 56, 448)), "y", 0, 0
    ).reshape(448, 448)

    def apply(block):
        return lax.dot_general(
            gram, block, (((0,), (0,)), ((), ())), preferred_element_type=f32
        ).reshape(2, 4, 56, 1664)

    once = spread(apply(rows_j), core)
    rows_once, total = ring_z(
        once.astype(bf16), total, (("y", 8, 1), ("y", 8, 2), ("y", 8, 4), ("x", 4, 1))
    )
    total, rows_once = lax.optimization_barrier((total, rows_once))
    total = add_swapped(total, "x", 4, 2)
    twice = spread(apply(rows_once), core)

    factor = math.sqrt(M) / 3.0 / (jnp.sqrt(total[0, 0]) + 1e-07)
    iterate = (momentum * factor).astype(bf16).astype(f32)
    small = factor / lift
    product = small * (small * (small * (coef_b * once + small * (small * (coef_c * twice)))))
    result = (coef_a * iterate + product) * (0.2 * math.sqrt(N))
    return result.astype(bf16)


def solution(mesh):
    fine = Mesh(mesh.devices.reshape(4, 8, 2, 8), ("x", "z", "c", "y"))
    spec = P(("x", "z", "c"), "y")
    return jax.shard_map(
        per_device, mesh=fine, in_specs=(spec,), out_specs=spec, check_vma=False
    )
```

```python
import math

import jax
import jax.numpy as jnp
from jax import lax
from jax.experimental import pallas as pl
from jax.experimental.pallas import tpu as pltpu
from jax.sharding import Mesh, PartitionSpec as P

M = 3584
N = 13312

coef_a = 3.4445
coef_b = -4.775
coef_c = 2.0315

bf16 = jnp.bfloat16
f32 = jnp.float32


def swap(size, bit):
    return [(i, i ^ bit) for i in range(size)]


def to_all(block, axis, size):
    return lax.all_to_all(jnp.broadcast_to(block[None], (size, *block.shape)), axis, 0, 0)


def other_core(block):
    return lax.ppermute(block, "c", swap(2, 1))


def add_swapped(total, steps):
    for axis, size, bit in steps:
        total = total + lax.ppermute(total, axis, swap(size, bit))
    return total


def rows_dot(left, right):
    return lax.dot_general(left, right, (((1,), (1,)), ((), ())), preferred_element_type=f32)


def depth_dot(left, right):
    return lax.dot_general(left, right, (((0,), (0,)), ((), ())), preferred_element_type=f32)


def split(value):
    high = lax.reduce_precision(value, 8, 7)
    middle = lax.reduce_precision(value - high, 8, 7)
    return high, middle, lax.reduce_precision(value - high - middle, 8, 7)


def in_lanes(lane, parts, rest):
    high, middle, low = parts
    return jnp.where(lane == 0, high, jnp.where(lane == 1, middle, jnp.where(lane == 2, low, rest)))


def local(kernel, out_shape, in_spaces, flops):
    spaces = [pl.BlockSpec(memory_space=space) for space in in_spaces]
    return pl.pallas_call(
        kernel,
        out_shape=out_shape,
        in_specs=spaces,
        out_specs=jax.tree.map(lambda _: pl.BlockSpec(memory_space=pltpu.VMEM), out_shape),
        compiler_params=pltpu.CompilerParams(vmem_limit_bytes=32 * 1024 * 1024),
        cost_estimate=pl.CostEstimate(flops=flops, bytes_accessed=3_000_000, transcendentals=0),
    )


def add_shares_kernel(shares_ref, piece_ref, copies_ref):
    summed = shares_ref[0].astype(f32)
    for share in range(1, 8):
        summed += shares_ref[share].astype(f32)
    total = jnp.sum(summed[:, 224:], axis=1, keepdims=True)
    high = total.astype(bf16).astype(f32)
    middle = (total - high).astype(bf16).astype(f32)
    lane = lax.broadcasted_iota(jnp.int32, (112, 256), 1) - 224
    rest = jnp.where(lane < 0, summed, 0.0)
    piece = in_lanes(lane, (high, middle, total - high - middle), rest).astype(bf16)
    piece_ref[...] = piece
    for share in range(8):
        copies_ref[share] = piece


def polynomial_kernel(left_ref, right_ref, gram_ref, poly_ref, factor_ref):
    square = jnp.zeros((112, 224), f32)
    lanes = jnp.zeros((112, 32), f32)
    for g in range(16):
        left = left_ref[g]
        square += jnp.dot(left[:, :224], right_ref[g][:, :224], preferred_element_type=f32)
        lanes += left[:, 224:].astype(f32)
    total = jnp.sum(lanes, axis=1, keepdims=True)
    factor = math.sqrt(M) / 3.0 / (jnp.sqrt(total) + 1e-07)
    factor2 = factor * factor
    gram = (gram_ref[:, :224].astype(f32) * factor2).astype(bf16).astype(f32)
    square = ((square * factor2) * factor2).astype(bf16).astype(f32)
    poly = (coef_b * gram + coef_c * square).astype(bf16)
    for g in range(8):
        poly_ref[g] = poly
    factor_ref[...] = jnp.broadcast_to(factor, (112, 128))


def update_kernel(momentum_ref, product_ref, factor_ref, update_ref):
    factor = factor_ref[:56, :1]
    product = product_ref[0].astype(f32)
    for x in range(1, 4):
        product += product_ref[x].astype(f32)
    iterate = (momentum_ref[...] * factor).astype(bf16).astype(f32)
    update = (coef_a * iterate + factor * product) * (0.2 * math.sqrt(N))
    update_ref[...] = update.astype(bf16)


def per_device(momentum):
    core = lax.axis_index("c")
    raw = momentum.astype(bf16)

    rows_own = to_all(raw, "z", 8).reshape(448, 1664)
    rows_x = lax.all_gather(raw, "x", axis=0, tiled=True)
    rows_x_other = other_core(rows_x)
    late, rows_x_other = lax.optimization_barrier((momentum, rows_x_other))
    total = jnp.broadcast_to(jnp.sum(late * late).reshape(1, 1), (8, 128))
    total = add_swapped(total, [("x", 4, 1), ("x", 4, 2)])
    lane = lax.broadcasted_iota(jnp.int32, (1, 32), 1)
    lanes = in_lanes(lane, split(total[:1, :32]), 0.0).astype(bf16)
    rows_own, rows_x, rows_x_other, lanes = lax.optimization_barrier(
        (rows_own, rows_x, rows_x_other, lanes)
    )

    part_own = rows_dot(rows_own, rows_x).astype(bf16).reshape(8, 1, 56, 224)
    part_given = rows_dot(rows_own, rows_x_other).astype(bf16)
    part_other = other_core(part_given).reshape(8, 1, 56, 224)
    part = jnp.where(
        core == 0,
        jnp.concatenate([part_own, part_other], axis=1),
        jnp.concatenate([part_other, part_own], axis=1),
    ).reshape(8, 112, 224)
    part = jnp.concatenate([part, jnp.broadcast_to(lanes[None], (8, 112, 32))], axis=2)
    piece, copies = local(
        add_shares_kernel,
        [jax.ShapeDtypeStruct((112, 256), bf16), jax.ShapeDtypeStruct((8, 112, 256), bf16)],
        [pltpu.VMEM],
        1_000_000,
    )(lax.all_to_all(part, "y", 0, 0))

    right = lax.all_to_all(copies, "y", 0, 0).reshape(8, 2, 56, 256)
    right, piece = lax.optimization_barrier((right, piece))
    right = to_all(right, "x", 4).transpose(1, 2, 0, 3, 4).reshape(16, 224, 256)
    left = lax.all_gather(piece, ("z", "c"), axis=0)
    poly, factor = local(
        polynomial_kernel,
        [jax.ShapeDtypeStruct((8, 112, 224), bf16), jax.ShapeDtypeStruct((112, 128), f32)],
        [pltpu.VMEM] * 3,
        2 * 112 * 224 * M,
    )(left, right, piece)

    poly, rows_own = lax.optimization_barrier((poly, rows_own))
    rows_other = other_core(rows_own)
    poly = lax.all_to_all(poly, "y", 0, 0).reshape(8, 2, 56, 224)
    poly_own = lax.dynamic_index_in_dim(poly, core, 1, keepdims=False).reshape(448, 224)
    poly_other = lax.dynamic_index_in_dim(poly, 1 - core, 1, keepdims=False).reshape(448, 224)
    product = depth_dot(poly_own, rows_own) + depth_dot(poly_other, rows_other)
    product = lax.all_to_all(product.astype(bf16).reshape(4, 56, 1664), "x", 0, 0)
    return local(
        update_kernel,
        jax.ShapeDtypeStruct((56, 1664), bf16),
        [pltpu.VMEM] * 3,
        1_000_000,
    )(momentum, product, factor)


def solution(mesh):
    fine = Mesh(mesh.devices.reshape(4, 8, 2, 8), ("x", "z", "c", "y"))
    spec = P(("x", "z", "c"), "y")
    return jax.shard_map(
        per_device, mesh=fine, in_specs=(spec,), out_specs=spec, check_vma=False
    )
```

```python
import math

import jax
import jax.numpy as jnp
from jax import lax
from jax.experimental import pallas as pl
from jax.experimental.pallas import tpu as pltpu
from jax.sharding import Mesh, PartitionSpec as P

M = 3584
N = 13312

coef_a = 3.4445
coef_b = -4.775
coef_c = 2.0315

bf16 = jnp.bfloat16
f32 = jnp.float32


def swap(size, bit):
    return [(i, i ^ bit) for i in range(size)]


def from_next_z(block):
    up = [(2 * z, 2 * ((z + 1) % 8)) for z in range(8)]
    down = [(2 * z + 1, 2 * ((z - 1) % 8) + 1) for z in range(8)]
    return lax.ppermute(block, ("zh", "zl", "c"), up + down)


def other_core(block):
    return lax.ppermute(block, "c", swap(2, 1))


def rows_dot(left, right):
    return lax.dot_general(left, right, (((1,), (1,)), ((), ())), preferred_element_type=f32)


def in_lanes(first, total, rest):
    high = total.astype(bf16).astype(f32)
    middle = (total - high).astype(bf16).astype(f32)
    lane = lax.broadcasted_iota(jnp.int32, rest.shape, 1) - first
    low = jnp.where(lane == 2, total - high - middle, rest)
    return jnp.where(lane == 0, high, jnp.where(lane == 1, middle, low))


def local(kernel, out_shape, in_spaces, flops):
    spaces = [pl.BlockSpec(memory_space=space) for space in in_spaces]
    return pl.pallas_call(
        kernel,
        out_shape=out_shape,
        in_specs=spaces,
        out_specs=jax.tree.map(lambda _: pl.BlockSpec(memory_space=pltpu.VMEM), out_shape),
        compiler_params=pltpu.CompilerParams(vmem_limit_bytes=32 * 1024 * 1024),
        cost_estimate=pl.CostEstimate(flops=flops, bytes_accessed=3_000_000, transcendentals=0),
    )


def start_kernel(momentum_ref, raw_ref, copies_ref):
    momentum = momentum_ref[...]
    raw = momentum.astype(bf16)
    for zh in range(4):
        copies_ref[zh] = raw
    total = jnp.sum(momentum * momentum, keepdims=True)
    more = in_lanes(0, jnp.broadcast_to(total, (8, 1664)), jnp.zeros((8, 1664), f32))
    raw_ref[...] = jnp.concatenate([momentum, more], axis=0).astype(bf16)


def copies_kernel(block_ref, copies_ref):
    for x in range(4):
        copies_ref[x] = block_ref[...]


def parts_kernel(place_ref, totals_ref, part_a_ref, part_b_ref, part_c_ref, rows_ref, rows_x_ref, parts_ref):
    zl, core = place_ref[0], place_ref[1]
    part_d = lax.dot_general(
        rows_ref[...], rows_x_ref[...], (((1,), (1,)), ((), ())), preferred_element_type=f32
    )
    total = jnp.zeros((8, 128), f32)
    for x in range(4):
        total += totals_ref[x, :, :128].astype(f32)[56:]
    total = jnp.sum(total[:1], axis=1, keepdims=True)
    lanes = in_lanes(0, jnp.broadcast_to(total, (56, 32)), jnp.zeros((56, 32), f32))
    for part, l, c in (
        (part_a_ref, zl, core),
        (part_b_ref, 1 - zl, core),
        (part_c_ref, zl, 1 - core),
        (part_d, 1 - zl, 1 - core),
    ):
        for zh in range(4):
            block = jnp.concatenate([part[56 * zh : 56 * zh + 56, :], lanes], axis=1)
            parts_ref[zh, l, c] = block.astype(bf16)


def product_kernel(place_ref, poly_ref, rows_a_ref, rows_b_ref, rows_c_ref, rows_d_ref, product_ref):
    zl, core = place_ref[0], place_ref[1]
    product = None
    for rows, l, c in (
        (rows_a_ref, zl, core),
        (rows_b_ref, 1 - zl, core),
        (rows_c_ref, zl, 1 - core),
        (rows_d_ref, 1 - zl, 1 - core),
    ):
        poly = jnp.concatenate([poly_ref[zh, l, c].astype(f32) for zh in range(4)], axis=0)
        term = lax.dot_general(
            poly.astype(bf16), rows[...], (((0,), (0,)), ((), ())), preferred_element_type=f32
        )
        product = term if product is None else product + term
    for x in range(4):
        product_ref[x] = product[56 * x : 56 * x + 56].astype(bf16)


def add_shares_kernel(shares_ref, piece_ref, copies_ref):
    summed = shares_ref[0].astype(f32)
    for share in range(1, 8):
        summed += shares_ref[share].astype(f32)
    total = jnp.sum(summed[:, 224:], axis=1, keepdims=True)
    lane = lax.broadcasted_iota(jnp.int32, (112, 256), 1)
    piece = in_lanes(224, total, jnp.where(lane < 224, summed, 0.0)).astype(bf16)
    piece_ref[...] = piece
    for share in range(8):
        copies_ref[share] = piece


def polynomial_kernel(left_ref, right_ref, gram_ref, poly_ref, factor_ref):
    square = jnp.zeros((112, 224), f32)
    lanes = jnp.zeros((112, 32), f32)
    for g in range(16):
        left = left_ref[g]
        right = jnp.concatenate(
            [right_ref[x, g // 2, g % 2].astype(f32) for x in range(4)], axis=0
        ).astype(bf16)
        square += jnp.dot(left[:, :224], right[:, :224], preferred_element_type=f32)
        lanes += left[:, 224:].astype(f32)
    total = jnp.sum(lanes, axis=1, keepdims=True)
    factor = math.sqrt(M) / 3.0 / (jnp.sqrt(total) + 1e-07)
    factor2 = factor * factor
    gram = (gram_ref[:, :224].astype(f32) * factor2).astype(bf16).astype(f32)
    square = ((square * factor2) * factor2).astype(bf16).astype(f32)
    poly = (coef_b * gram + coef_c * square).astype(bf16)
    for g in range(8):
        poly_ref[g] = poly
    factor_ref[...] = jnp.broadcast_to(factor, (112, 128))


def update_kernel(momentum_ref, product_ref, factor_ref, update_ref):
    factor = factor_ref[:56, :1]
    product = product_ref[0].astype(f32)
    for x in range(1, 4):
        product += product_ref[x].astype(f32)
    iterate = (momentum_ref[...] * factor).astype(bf16).astype(f32)
    update = (coef_a * iterate + factor * product) * (0.2 * math.sqrt(N))
    update_ref[...] = update.astype(bf16)


def per_device(momentum):
    place = jnp.stack([lax.axis_index("zl"), lax.axis_index("c")]).astype(jnp.int32)
    raw, copies = local(
        start_kernel,
        [jax.ShapeDtypeStruct((64, 1664), bf16), jax.ShapeDtypeStruct((4, 56, 1664), bf16)],
        [pltpu.VMEM],
        1_000_000,
    )(momentum)

    rows_a = lax.all_to_all(copies, "zh", 0, 0).reshape(224, 1664)
    gathered_x = lax.all_gather(raw, "x", axis=0)
    rows_x = gathered_x[:, :56].reshape(224, 1664)
    rows_a, rows_x = lax.optimization_barrier((rows_a, rows_x))
    rows_b = from_next_z(rows_a)
    rows_c = other_core(rows_a)
    rows_d = other_core(rows_b)

    parts = local(
        parts_kernel,
        jax.ShapeDtypeStruct((4, 2, 2, 56, 256), bf16),
        [pltpu.SMEM] + [pltpu.VMEM] * 6,
        2 * 224 * 224 * 1664,
    )(
        place,
        gathered_x[:, :, :128],
        *(rows_dot(rows, rows_x) for rows in (rows_a, rows_b, rows_c)),
        rows_d,
        rows_x,
    )
    piece, copies = local(
        add_shares_kernel,
        [jax.ShapeDtypeStruct((112, 256), bf16), jax.ShapeDtypeStruct((8, 112, 256), bf16)],
        [pltpu.VMEM],
        1_000_000,
    )(lax.all_to_all(parts.reshape(8, 112, 256), "y", 0, 0))

    right = lax.all_to_all(copies, "y", 0, 0)
    right, piece = lax.optimization_barrier((right, piece))
    copies = local(
        copies_kernel, jax.ShapeDtypeStruct((4, 8, 112, 256), bf16), [pltpu.VMEM], 1_000_000
    )(right)
    right = lax.all_to_all(copies, "x", 0, 0).reshape(4, 8, 2, 56, 256)
    left = lax.all_gather(piece, ("zh", "zl", "c"), axis=0)
    poly, factor = local(
        polynomial_kernel,
        [jax.ShapeDtypeStruct((8, 112, 224), bf16), jax.ShapeDtypeStruct((112, 128), f32)],
        [pltpu.VMEM] * 3,
        2 * 112 * 224 * M,
    )(left, right, piece)

    poly = lax.all_to_all(poly, "y", 0, 0).reshape(4, 2, 2, 56, 224)
    product = local(
        product_kernel,
        jax.ShapeDtypeStruct((4, 56, 1664), bf16),
        [pltpu.SMEM] + [pltpu.VMEM] * 5,
        2 * 896 * 224 * 1664,
    )(place, poly, rows_a, rows_b, rows_c, rows_d)
    return local(
        update_kernel,
        jax.ShapeDtypeStruct((56, 1664), bf16),
        [pltpu.VMEM] * 3,
        1_000_000,
    )(momentum, lax.all_to_all(product, "x", 0, 0), factor)


def solution(mesh):
    names = ("x", "zh", "zl", "c", "y")
    fine = Mesh(mesh.devices.reshape(4, 4, 2, 2, 8), names)
    spec = P(names[:4], "y")
    return jax.shard_map(
        per_device, mesh=fine, in_specs=(spec,), out_specs=spec, check_vma=False
    )
```

```python
import math

import jax
import jax.numpy as jnp
from jax import lax
from jax.experimental import pallas as pl
from jax.experimental.pallas import tpu as pltpu
from jax.sharding import Mesh, PartitionSpec as P

M = 3584
N = 13312

coef_a = 3.4445
coef_b = -4.775
coef_c = 2.0315

bf16 = jnp.bfloat16
f32 = jnp.float32


def swap(size, bit):
    return [(i, i ^ bit) for i in range(size)]


def from_next_z(block):
    up = [(2 * z, 2 * ((z + 1) % 8)) for z in range(8)]
    down = [(2 * z + 1, 2 * ((z - 1) % 8) + 1) for z in range(8)]
    return lax.ppermute(block, ("zh", "zl", "c"), up + down)


def other_core(block):
    return lax.ppermute(block, "c", swap(2, 1))


def rows_dot(left, right):
    return lax.dot_general(left, right, (((1,), (1,)), ((), ())), preferred_element_type=f32)


def in_lanes(first, total, rest):
    high = total.astype(bf16).astype(f32)
    middle = (total - high).astype(bf16).astype(f32)
    lane = lax.broadcasted_iota(jnp.int32, rest.shape, 1) - first
    low = jnp.where(lane == 2, total - high - middle, rest)
    return jnp.where(lane == 0, high, jnp.where(lane == 1, middle, low))


def local(kernel, out_shape, in_spaces, flops):
    spaces = [pl.BlockSpec(memory_space=space) for space in in_spaces]
    return pl.pallas_call(
        kernel,
        out_shape=out_shape,
        in_specs=spaces,
        out_specs=jax.tree.map(lambda _: pl.BlockSpec(memory_space=pltpu.VMEM), out_shape),
        compiler_params=pltpu.CompilerParams(vmem_limit_bytes=32 * 1024 * 1024),
        cost_estimate=pl.CostEstimate(flops=flops, bytes_accessed=3_000_000, transcendentals=0),
    )


def start_kernel(momentum_ref, raw_ref, copies_ref):
    momentum = momentum_ref[...]
    raw_ref[...] = momentum.astype(bf16)
    total = jnp.sum(momentum * momentum, keepdims=True)
    more = in_lanes(0, jnp.broadcast_to(total, (8, 1664)), jnp.zeros((8, 1664), f32))
    longer = jnp.concatenate([momentum, more], axis=0).astype(bf16)
    for x in range(4):
        copies_ref[x] = longer


def copies_kernel(block_ref, copies_ref):
    for x in range(4):
        copies_ref[x] = block_ref[...]


def parts_kernel(place_ref, totals_ref, part_a_ref, part_b_ref, part_c_ref, rows_ref, rows_x_ref, parts_ref):
    zl, core = place_ref[0], place_ref[1]
    part_d = lax.dot_general(
        rows_ref[...], rows_x_ref[...], (((1,), (1,)), ((), ())), preferred_element_type=f32
    )
    total = jnp.zeros((8, 128), f32)
    for x in range(4):
        total += totals_ref[x, :, :128].astype(f32)[56:]
    total = jnp.sum(total[:1], axis=1, keepdims=True)
    lanes = in_lanes(0, jnp.broadcast_to(total, (56, 32)), jnp.zeros((56, 32), f32))
    for part, l, c in (
        (part_a_ref, zl, core),
        (part_b_ref, 1 - zl, core),
        (part_c_ref, zl, 1 - core),
        (part_d, 1 - zl, 1 - core),
    ):
        for zh in range(4):
            block = jnp.concatenate([part[56 * zh : 56 * zh + 56, :], lanes], axis=1)
            parts_ref[zh, l, c] = block.astype(bf16)


def product_kernel(place_ref, poly_ref, rows_a_ref, rows_b_ref, rows_c_ref, rows_d_ref, product_ref):
    zl, core = place_ref[0], place_ref[1]
    product = None
    for rows, l, c in (
        (rows_a_ref, zl, core),
        (rows_b_ref, 1 - zl, core),
        (rows_c_ref, zl, 1 - core),
        (rows_d_ref, 1 - zl, 1 - core),
    ):
        poly = jnp.concatenate([poly_ref[zh, l, c].astype(f32) for zh in range(4)], axis=0)
        term = lax.dot_general(
            poly.astype(bf16), rows[...], (((0,), (0,)), ((), ())), preferred_element_type=f32
        )
        product = term if product is None else product + term
    for x in range(4):
        product_ref[x] = product[56 * x : 56 * x + 56].astype(bf16)


def add_shares_kernel(shares_ref, piece_ref, copies_ref):
    summed = shares_ref[0].astype(f32)
    for share in range(1, 8):
        summed += shares_ref[share].astype(f32)
    total = jnp.sum(summed[:, 224:], axis=1, keepdims=True)
    lane = lax.broadcasted_iota(jnp.int32, (112, 256), 1)
    piece = in_lanes(224, total, jnp.where(lane < 224, summed, 0.0)).astype(bf16)
    piece_ref[...] = piece
    for share in range(8):
        copies_ref[share] = piece


def polynomial_kernel(left_ref, right_ref, gram_ref, poly_ref, factor_ref):
    square = jnp.zeros((112, 224), f32)
    lanes = jnp.zeros((112, 32), f32)
    for g in range(16):
        left = left_ref[g]
        right = jnp.concatenate(
            [right_ref[x, g // 2, g % 2].astype(f32) for x in range(4)], axis=0
        ).astype(bf16)
        square += jnp.dot(left[:, :224], right[:, :224], preferred_element_type=f32)
        lanes += left[:, 224:].astype(f32)
    total = jnp.sum(lanes, axis=1, keepdims=True)
    factor = math.sqrt(M) / 3.0 / (jnp.sqrt(total) + 1e-07)
    factor2 = factor * factor
    gram = (gram_ref[:, :224].astype(f32) * factor2).astype(bf16).astype(f32)
    square = ((square * factor2) * factor2).astype(bf16).astype(f32)
    poly = (coef_b * gram + coef_c * square).astype(bf16)
    for g in range(8):
        poly_ref[g] = poly
    factor_ref[...] = jnp.broadcast_to(factor, (112, 128))


def update_kernel(momentum_ref, product_ref, factor_ref, update_ref):
    factor = factor_ref[:56, :1]
    product = product_ref[0].astype(f32)
    for x in range(1, 4):
        product += product_ref[x].astype(f32)
    iterate = (momentum_ref[...] * factor).astype(bf16).astype(f32)
    update = (coef_a * iterate + factor * product) * (0.2 * math.sqrt(N))
    update_ref[...] = update.astype(bf16)


def per_device(momentum):
    place = jnp.stack([lax.axis_index("zl"), lax.axis_index("c")]).astype(jnp.int32)
    short, copies = local(
        start_kernel,
        [jax.ShapeDtypeStruct((56, 1664), bf16), jax.ShapeDtypeStruct((4, 64, 1664), bf16)],
        [pltpu.VMEM],
        1_000_000,
    )(momentum)

    rows_a = lax.all_gather(short, "zh", axis=0, tiled=True)
    rows_a, copies = lax.optimization_barrier((rows_a, copies))
    gathered_x = lax.all_to_all(copies, "x", 0, 0)
    rows_x = gathered_x[:, :56].reshape(224, 1664)
    rows_b = from_next_z(rows_a)
    rows_c = other_core(rows_a)
    rows_d = other_core(rows_b)

    parts = local(
        parts_kernel,
        jax.ShapeDtypeStruct((4, 2, 2, 56, 256), bf16),
        [pltpu.SMEM] + [pltpu.VMEM] * 6,
        2 * 224 * 224 * 1664,
    )(
        place,
        gathered_x[:, :, :128],
        *(rows_dot(rows, rows_x) for rows in (rows_a, rows_b, rows_c)),
        rows_d,
        rows_x,
    )
    piece, copies = local(
        add_shares_kernel,
        [jax.ShapeDtypeStruct((112, 256), bf16), jax.ShapeDtypeStruct((8, 112, 256), bf16)],
        [pltpu.VMEM],
        1_000_000,
    )(lax.all_to_all(parts.reshape(8, 112, 256), "y", 0, 0))

    right = lax.all_to_all(copies, "y", 0, 0)
    right, piece = lax.optimization_barrier((right, piece))
    copies = local(
        copies_kernel, jax.ShapeDtypeStruct((4, 8, 112, 256), bf16), [pltpu.VMEM], 1_000_000
    )(right)
    right = lax.all_to_all(copies, "x", 0, 0).reshape(4, 8, 2, 56, 256)
    left = lax.all_gather(piece, ("zh", "zl", "c"), axis=0)
    poly, factor = local(
        polynomial_kernel,
        [jax.ShapeDtypeStruct((8, 112, 224), bf16), jax.ShapeDtypeStruct((112, 128), f32)],
        [pltpu.VMEM] * 3,
        2 * 112 * 224 * M,
    )(left, right, piece)

    poly = lax.all_to_all(poly, "y", 0, 0).reshape(4, 2, 2, 56, 224)
    product = local(
        product_kernel,
        jax.ShapeDtypeStruct((4, 56, 1664), bf16),
        [pltpu.SMEM] + [pltpu.VMEM] * 5,
        2 * 896 * 224 * 1664,
    )(place, poly, rows_a, rows_b, rows_c, rows_d)
    return local(
        update_kernel,
        jax.ShapeDtypeStruct((56, 1664), bf16),
        [pltpu.VMEM] * 3,
        1_000_000,
    )(momentum, lax.all_to_all(product, "x", 0, 0), factor)


def solution(mesh):
    names = ("x", "zh", "zl", "c", "y")
    fine = Mesh(mesh.devices.reshape(4, 4, 2, 2, 8), names)
    spec = P(names[:4], "y")
    return jax.shard_map(
        per_device, mesh=fine, in_specs=(spec,), out_specs=spec, check_vma=False
    )
```

```python
import math

import jax
import jax.numpy as jnp
from jax import lax
from jax.experimental import pallas as pl
from jax.experimental.pallas import tpu as pltpu
from jax.sharding import Mesh, PartitionSpec as P

M = 3584
N = 13312

coef_a = 3.4445
coef_b = -4.775
coef_c = 2.0315

bf16 = jnp.bfloat16
f32 = jnp.float32


def swap(size, bit):
    return [(i, i ^ bit) for i in range(size)]


def from_next_z(block):
    up = [(2 * z, 2 * ((z + 1) % 8)) for z in range(8)]
    down = [(2 * z + 1, 2 * ((z - 1) % 8) + 1) for z in range(8)]
    return lax.ppermute(block, ("zh", "zl", "c"), up + down)


def other_core(block):
    return lax.ppermute(block, "c", swap(2, 1))


def rows_dot(left, right):
    return lax.dot_general(left, right, (((1,), (1,)), ((), ())), preferred_element_type=f32)


def in_lanes(first, total, rest):
    high = total.astype(bf16).astype(f32)
    middle = (total - high).astype(bf16).astype(f32)
    lane = lax.broadcasted_iota(jnp.int32, rest.shape, 1) - first
    low = jnp.where(lane == 2, total - high - middle, rest)
    return jnp.where(lane == 0, high, jnp.where(lane == 1, middle, low))


def local(kernel, out_shape, in_spaces, flops):
    spaces = [pl.BlockSpec(memory_space=space) for space in in_spaces]
    return pl.pallas_call(
        kernel,
        out_shape=out_shape,
        in_specs=spaces,
        out_specs=jax.tree.map(lambda _: pl.BlockSpec(memory_space=pltpu.VMEM), out_shape),
        compiler_params=pltpu.CompilerParams(vmem_limit_bytes=32 * 1024 * 1024),
        cost_estimate=pl.CostEstimate(flops=flops, bytes_accessed=3_000_000, transcendentals=0),
    )


def start_kernel(momentum_ref, raw_ref, copies_ref):
    momentum = momentum_ref[...]
    raw_ref[...] = momentum.astype(bf16)
    total = jnp.sum(momentum * momentum, keepdims=True)
    more = in_lanes(0, jnp.broadcast_to(total, (8, 1664)), jnp.zeros((8, 1664), f32))
    longer = jnp.concatenate([momentum, more], axis=0).astype(bf16)
    for x in range(4):
        copies_ref[x] = longer


def copies_kernel(block_ref, copies_ref):
    for x in range(4):
        copies_ref[x] = block_ref[...]


def pack(block, total):
    high = block[:, 128:]
    rest = high[88:]
    if total is None:
        spare = jnp.zeros((16, 32), f32)
    else:
        spare = in_lanes(0, jnp.broadcast_to(total, (16, 32)), jnp.zeros((16, 32), f32))
    beside = jnp.concatenate([rest[:, :32], rest[:, 32:64], rest[:, 64:], spare], axis=0)
    below = jnp.concatenate([high[:88], beside], axis=1)
    return jnp.concatenate([block[:, :128], below], axis=0)


def unpack(packed):
    beside = packed[112:, 96:]
    rest = jnp.concatenate([beside[:24], beside[24:48], beside[48:72]], axis=1)
    high = jnp.concatenate([packed[112:, :96], rest], axis=0)
    return jnp.concatenate([packed[:112], high], axis=1)


def packed_total(packed):
    return jnp.sum(packed[184:192, 96:][:1], axis=1, keepdims=True)


def parts_kernel(place_ref, totals_ref, part_a_ref, part_b_ref, part_c_ref, rows_ref, rows_x_ref, parts_ref):
    zl, first = place_ref[0], place_ref[1] == 0
    part_d = lax.dot_general(
        rows_ref[...], rows_x_ref[...], (((1,), (1,)), ((), ())), preferred_element_type=f32
    )
    total = jnp.zeros((8, 128), f32)
    for x in range(4):
        total += totals_ref[x, :, :128].astype(f32)[56:]
    total = jnp.sum(total[:1], axis=1, keepdims=True)
    for own, other, l in ((part_a_ref, part_c_ref, zl), (part_b_ref, part_d, 1 - zl)):
        for zh in range(4):
            mine, its = own[56 * zh : 56 * zh + 56, :], other[56 * zh : 56 * zh + 56, :]
            block = jnp.concatenate(
                [jnp.where(first, mine, its), jnp.where(first, its, mine)], axis=0
            )
            parts_ref[2 * zh + l] = pack(block, total).astype(bf16)


def add_shares_kernel(shares_ref, piece_ref, copies_ref):
    summed = shares_ref[0].astype(f32)
    for share in range(1, 8):
        summed += shares_ref[share].astype(f32)
    row = lax.broadcasted_iota(jnp.int32, (200, 128), 0)
    with_total = in_lanes(96, packed_total(summed), summed)
    piece = jnp.where(row >= 184, with_total, summed).astype(bf16)
    piece_ref[...] = piece
    for share in range(8):
        copies_ref[share] = piece


def polynomial_kernel(left_ref, right_ref, gram_ref, poly_ref, factor_ref):
    square = jnp.zeros((112, 224), f32)
    total = jnp.zeros((1, 1), f32)
    for z in range(8):
        rights = [unpack(right_ref[x, z].astype(f32)) for x in range(4)]
        for c in range(2):
            left = left_ref[2 * z + c].astype(f32)
            total += packed_total(left)
            right = jnp.concatenate([block[56 * c : 56 * c + 56] for block in rights], axis=0)
            square += jnp.dot(
                unpack(left).astype(bf16), right.astype(bf16), preferred_element_type=f32
            )
    factor = math.sqrt(M) / 3.0 / (jnp.sqrt(total) + 1e-07)
    factor2 = factor * factor
    gram = (unpack(gram_ref[...].astype(f32)) * factor2).astype(bf16).astype(f32)
    square = ((square * factor2) * factor2).astype(bf16).astype(f32)
    poly = pack(coef_b * gram + coef_c * square, None).astype(bf16)
    for share in range(8):
        poly_ref[share] = poly
    factor_ref[...] = jnp.broadcast_to(factor, (8, 128))


def product_kernel(place_ref, poly_ref, rows_a_ref, rows_b_ref, rows_c_ref, rows_d_ref, product_ref):
    zl, first = place_ref[0], place_ref[1] == 0
    product = None
    for own, other, l in ((rows_a_ref, rows_c_ref, zl), (rows_b_ref, rows_d_ref, 1 - zl)):
        blocks = [unpack(poly_ref[2 * zh + l].astype(f32)) for zh in range(4)]
        lower = jnp.concatenate([block[:56] for block in blocks], axis=0)
        upper = jnp.concatenate([block[56:] for block in blocks], axis=0)
        for rows, poly in (
            (own, jnp.where(first, lower, upper)),
            (other, jnp.where(first, upper, lower)),
        ):
            term = lax.dot_general(
                poly.astype(bf16), rows[...], (((0,), (0,)), ((), ())), preferred_element_type=f32
            )
            product = term if product is None else product + term
    for x in range(4):
        product_ref[x] = product[56 * x : 56 * x + 56].astype(bf16)


def update_kernel(momentum_ref, product_ref, factor_ref, update_ref):
    factor = factor_ref[:1, :1]
    product = product_ref[0].astype(f32)
    for x in range(1, 4):
        product += product_ref[x].astype(f32)
    iterate = (momentum_ref[...] * factor).astype(bf16).astype(f32)
    update = (coef_a * iterate + factor * product) * (0.2 * math.sqrt(N))
    update_ref[...] = update.astype(bf16)


def per_device(momentum):
    place = jnp.stack([lax.axis_index("zl"), lax.axis_index("c")]).astype(jnp.int32)
    short, copies = local(
        start_kernel,
        [jax.ShapeDtypeStruct((56, 1664), bf16), jax.ShapeDtypeStruct((4, 64, 1664), bf16)],
        [pltpu.VMEM],
        1_000_000,
    )(momentum)

    rows_a = lax.all_gather(short, "zh", axis=0, tiled=True)
    rows_a, copies = lax.optimization_barrier((rows_a, copies))
    gathered_x = lax.all_to_all(copies, "x", 0, 0)
    rows_x = gathered_x[:, :56].reshape(224, 1664)
    rows_b = from_next_z(rows_a)
    rows_c = other_core(rows_a)
    rows_d = other_core(rows_b)

    parts = local(
        parts_kernel,
        jax.ShapeDtypeStruct((8, 200, 128), bf16),
        [pltpu.SMEM] + [pltpu.VMEM] * 6,
        2 * 224 * 224 * 1664,
    )(
        place,
        gathered_x[:, :, :128],
        *(rows_dot(rows, rows_x) for rows in (rows_a, rows_b, rows_c)),
        rows_d,
        rows_x,
    )
    piece, copies = local(
        add_shares_kernel,
        [jax.ShapeDtypeStruct((200, 128), bf16), jax.ShapeDtypeStruct((8, 200, 128), bf16)],
        [pltpu.VMEM],
        1_000_000,
    )(lax.all_to_all(parts, "y", 0, 0))

    right = lax.all_to_all(copies, "y", 0, 0)
    right, piece = lax.optimization_barrier((right, piece))
    copies = local(
        copies_kernel, jax.ShapeDtypeStruct((4, 8, 200, 128), bf16), [pltpu.VMEM], 1_000_000
    )(right)
    right = lax.all_to_all(copies, "x", 0, 0)
    left = lax.all_gather(piece, ("zh", "zl", "c"), axis=0)
    poly, factor = local(
        polynomial_kernel,
        [jax.ShapeDtypeStruct((8, 200, 128), bf16), jax.ShapeDtypeStruct((8, 128), f32)],
        [pltpu.VMEM] * 3,
        2 * 112 * 224 * M,
    )(left, right, piece)

    poly = lax.all_to_all(poly, "y", 0, 0)
    product = local(
        product_kernel,
        jax.ShapeDtypeStruct((4, 56, 1664), bf16),
        [pltpu.SMEM] + [pltpu.VMEM] * 5,
        2 * 896 * 224 * 1664,
    )(place, poly, rows_a, rows_b, rows_c, rows_d)
    return local(
        update_kernel,
        jax.ShapeDtypeStruct((56, 1664), bf16),
        [pltpu.VMEM] * 3,
        1_000_000,
    )(momentum, lax.all_to_all(product, "x", 0, 0), factor)


def solution(mesh):
    names = ("x", "zh", "zl", "c", "y")
    fine = Mesh(mesh.devices.reshape(4, 4, 2, 2, 8), names)
    spec = P(names[:4], "y")
    return jax.shard_map(
        per_device, mesh=fine, in_specs=(spec,), out_specs=spec, check_vma=False
    )
```

```python
import math

import jax
import jax.numpy as jnp
from jax import lax
from jax.experimental import pallas as pl
from jax.experimental.pallas import tpu as pltpu
from jax.sharding import Mesh, PartitionSpec as P

M = 3584
N = 13312

coef_a = 3.4445
coef_b = -4.775
coef_c = 2.0315

lift = 2.0**14

bf16 = jnp.bfloat16
f32 = jnp.float32


def swap(size, bit):
    return [(i, i ^ bit) for i in range(size)]


def from_next_z(block):
    up = [(2 * z, 2 * ((z + 1) % 8)) for z in range(8)]
    down = [(2 * z + 1, 2 * ((z - 1) % 8) + 1) for z in range(8)]
    return lax.ppermute(block, ("zh", "zl", "c"), up + down)


def other_core(block):
    return lax.ppermute(block, "c", swap(2, 1))


def rows_dot(left, right):
    return lax.dot_general(left, right, (((1,), (1,)), ((), ())), preferred_element_type=f32)


def in_lanes(first, total, rest):
    high = total.astype(bf16).astype(f32)
    middle = (total - high).astype(bf16).astype(f32)
    lane = lax.broadcasted_iota(jnp.int32, rest.shape, 1) - first
    low = jnp.where(lane == 2, total - high - middle, rest)
    return jnp.where(lane == 0, high, jnp.where(lane == 1, middle, low))


def local(kernel, out_shape, in_spaces, flops):
    spaces = [pl.BlockSpec(memory_space=space) for space in in_spaces]
    return pl.pallas_call(
        kernel,
        out_shape=out_shape,
        in_specs=spaces,
        out_specs=jax.tree.map(lambda _: pl.BlockSpec(memory_space=pltpu.VMEM), out_shape),
        compiler_params=pltpu.CompilerParams(vmem_limit_bytes=32 * 1024 * 1024),
        cost_estimate=pl.CostEstimate(flops=flops, bytes_accessed=3_000_000, transcendentals=0),
    )


def start_kernel(momentum_ref, raw_ref, copies_ref):
    momentum = momentum_ref[...]
    lifted = momentum * lift
    raw_ref[...] = lifted.astype(bf16)
    total = jnp.sum(momentum * momentum, keepdims=True)
    more = in_lanes(0, jnp.broadcast_to(total, (8, 1664)), jnp.zeros((8, 1664), f32))
    longer = jnp.concatenate([lifted, more], axis=0).astype(bf16)
    for x in range(4):
        copies_ref[x] = longer


def copies_kernel(block_ref, copies_ref):
    for x in range(4):
        copies_ref[x] = block_ref[...]


def pack(block, total):
    high = block[:, 128:]
    rest = high[88:]
    if total is None:
        spare = jnp.zeros((16, 32), f32)
    else:
        spare = in_lanes(0, jnp.broadcast_to(total, (16, 32)), jnp.zeros((16, 32), f32))
    beside = jnp.concatenate([rest[:, :32], rest[:, 32:64], rest[:, 64:], spare], axis=0)
    below = jnp.concatenate([high[:88], beside], axis=1)
    return jnp.concatenate([block[:, :128], below], axis=0)


def unpack(packed):
    beside = packed[112:, 96:]
    rest = jnp.concatenate([beside[:24], beside[24:48], beside[48:72]], axis=1)
    high = jnp.concatenate([packed[112:, :96], rest], axis=0)
    return jnp.concatenate([packed[:112], high], axis=1)


def packed_total(packed):
    return jnp.sum(packed[184:192, 96:][:1], axis=1, keepdims=True)


def parts_kernel(place_ref, totals_ref, part_a_ref, part_b_ref, part_c_ref, rows_ref, rows_x_ref, parts_ref):
    zl, first = place_ref[0], place_ref[1] == 0
    part_d = lax.dot_general(
        rows_ref[...], rows_x_ref[...], (((1,), (1,)), ((), ())), preferred_element_type=f32
    )
    total = jnp.zeros((8, 128), f32)
    for x in range(4):
        total += totals_ref[x, :, :128].astype(f32)[56:]
    total = jnp.sum(total[:1], axis=1, keepdims=True)
    for own, other, l in ((part_a_ref, part_c_ref, zl), (part_b_ref, part_d, 1 - zl)):
        for zh in range(4):
            mine, its = own[56 * zh : 56 * zh + 56, :], other[56 * zh : 56 * zh + 56, :]
            block = jnp.concatenate(
                [jnp.where(first, mine, its), jnp.where(first, its, mine)], axis=0
            )
            parts_ref[2 * zh + l] = pack(block, total).astype(bf16)


def add_shares_kernel(shares_ref, piece_ref, copies_ref):
    summed = shares_ref[0].astype(f32)
    for share in range(1, 8):
        summed += shares_ref[share].astype(f32)
    row = lax.broadcasted_iota(jnp.int32, (200, 128), 0)
    with_total = in_lanes(96, packed_total(summed), summed)
    piece = jnp.where(row >= 184, with_total, summed).astype(bf16)
    piece_ref[...] = piece
    for share in range(8):
        copies_ref[share] = piece


def polynomial_kernel(left_ref, right_ref, gram_ref, poly_ref, factor_ref):
    square = jnp.zeros((112, 224), f32)
    total = jnp.zeros((1, 1), f32)
    for z in range(8):
        rights = [unpack(right_ref[x, z].astype(f32)) for x in range(4)]
        for c in range(2):
            left = left_ref[2 * z + c].astype(f32)
            total += packed_total(left)
            right = jnp.concatenate([block[56 * c : 56 * c + 56] for block in rights], axis=0)
            square += jnp.dot(
                unpack(left).astype(bf16), right.astype(bf16), preferred_element_type=f32
            )
    factor = math.sqrt(M) / 3.0 / (jnp.sqrt(total) + 1e-07)
    factor2 = (factor / lift) * (factor / lift)
    gram = (unpack(gram_ref[...].astype(f32)) * factor2).astype(bf16).astype(f32)
    square = ((square * factor2) * factor2).astype(bf16).astype(f32)
    poly = pack(coef_b * gram + coef_c * square, None).astype(bf16)
    for share in range(8):
        poly_ref[share] = poly
    factor_ref[...] = jnp.broadcast_to(factor, (8, 128))


def product_kernel(place_ref, poly_ref, rows_a_ref, rows_b_ref, rows_c_ref, rows_d_ref, product_ref, diagonal_ref):
    zl, first = place_ref[0], place_ref[1] == 0
    product = None
    for own, other, l in ((rows_a_ref, rows_c_ref, zl), (rows_b_ref, rows_d_ref, 1 - zl)):
        blocks = [unpack(poly_ref[2 * zh + l].astype(f32)) for zh in range(4)]
        lower = jnp.concatenate([block[:56] for block in blocks], axis=0)
        upper = jnp.concatenate([block[56:] for block in blocks], axis=0)
        for rows, poly in (
            (own, jnp.where(first, lower, upper)),
            (other, jnp.where(first, upper, lower)),
        ):
            term = lax.dot_general(
                poly.astype(bf16), rows[...], (((0,), (0,)), ((), ())), preferred_element_type=f32
            )
            product = term if product is None else product + term
    for x in range(4):
        product_ref[x] = product[56 * x : 56 * x + 56].astype(bf16)
    block = unpack(poly_ref[2 * place_ref[2] + zl].astype(f32))
    block = jnp.where(first, block[:56], block[56:])
    row = lax.broadcasted_iota(jnp.int32, (56, 224), 0)
    lane = lax.broadcasted_iota(jnp.int32, (56, 224), 1)
    diagonal = jnp.where(lane == row + 56 * place_ref[3], block, 0.0)
    diagonal_ref[...] = jnp.broadcast_to(jnp.sum(diagonal, axis=1, keepdims=True), (56, 128))


def update_kernel(momentum_ref, product_ref, diagonal_ref, factor_ref, update_ref):
    factor = factor_ref[:1, :1]
    product = product_ref[0].astype(f32)
    for x in range(1, 4):
        product += product_ref[x].astype(f32)
    momentum = momentum_ref[...]
    iterate = (momentum * factor).astype(bf16).astype(f32)
    small = factor / lift
    change = iterate - small * (momentum * lift).astype(bf16).astype(f32)
    product = small * product + diagonal_ref[:, :1] * change
    update_ref[...] = ((coef_a * iterate + product) * (0.2 * math.sqrt(N))).astype(bf16)


def per_device(momentum):
    place = jnp.stack([lax.axis_index(name) for name in ("zl", "c", "zh", "x")]).astype(jnp.int32)
    short, copies = local(
        start_kernel,
        [jax.ShapeDtypeStruct((56, 1664), bf16), jax.ShapeDtypeStruct((4, 64, 1664), bf16)],
        [pltpu.VMEM],
        1_000_000,
    )(momentum)

    rows_a = lax.all_gather(short, "zh", axis=0, tiled=True)
    rows_a, copies = lax.optimization_barrier((rows_a, copies))
    gathered_x = lax.all_to_all(copies, "x", 0, 0)
    rows_x = gathered_x[:, :56].reshape(224, 1664)
    rows_b = from_next_z(rows_a)
    rows_c = other_core(rows_a)
    rows_d = other_core(rows_b)

    parts = local(
        parts_kernel,
        jax.ShapeDtypeStruct((8, 200, 128), bf16),
        [pltpu.SMEM] + [pltpu.VMEM] * 6,
        2 * 224 * 224 * 1664,
    )(
        place,
        gathered_x[:, :, :128],
        *(rows_dot(rows, rows_x) for rows in (rows_a, rows_b, rows_c)),
        rows_d,
        rows_x,
    )
    piece, copies = local(
        add_shares_kernel,
        [jax.ShapeDtypeStruct((200, 128), bf16), jax.ShapeDtypeStruct((8, 200, 128), bf16)],
        [pltpu.VMEM],
        1_000_000,
    )(lax.all_to_all(parts, "y", 0, 0))

    right = lax.all_to_all(copies, "y", 0, 0)
    right, piece = lax.optimization_barrier((right, piece))
    copies = local(
        copies_kernel, jax.ShapeDtypeStruct((4, 8, 200, 128), bf16), [pltpu.VMEM], 1_000_000
    )(right)
    right = lax.all_to_all(copies, "x", 0, 0)
    left = lax.all_gather(piece, ("zh", "zl", "c"), axis=0)
    poly, factor = local(
        polynomial_kernel,
        [jax.ShapeDtypeStruct((8, 200, 128), bf16), jax.ShapeDtypeStruct((8, 128), f32)],
        [pltpu.VMEM] * 3,
        2 * 112 * 224 * M,
    )(left, right, piece)

    poly = lax.all_to_all(poly, "y", 0, 0)
    product, diagonal = local(
        product_kernel,
        [jax.ShapeDtypeStruct((4, 56, 1664), bf16), jax.ShapeDtypeStruct((56, 128), f32)],
        [pltpu.SMEM] + [pltpu.VMEM] * 5,
        2 * 896 * 224 * 1664,
    )(place, poly, rows_a, rows_b, rows_c, rows_d)
    return local(
        update_kernel,
        jax.ShapeDtypeStruct((56, 1664), bf16),
        [pltpu.VMEM] * 4,
        1_000_000,
    )(momentum, lax.all_to_all(product, "x", 0, 0), diagonal, factor)


def solution(mesh):
    names = ("x", "zh", "zl", "c", "y")
    fine = Mesh(mesh.devices.reshape(4, 4, 2, 2, 8), names)
    spec = P(names[:4], "y")
    return jax.shard_map(
        per_device, mesh=fine, in_specs=(spec,), out_specs=spec, check_vma=False
    )
```

```python
import math

import jax
import jax.numpy as jnp
from jax import lax
from jax.experimental import pallas as pl
from jax.experimental.pallas import tpu as pltpu
from jax.sharding import Mesh, PartitionSpec as P

M = 3584
N = 13312

coef_a = 3.4445
coef_b = -4.775
coef_c = 2.0315

lift = 2.0**14

bf16 = jnp.bfloat16
f32 = jnp.float32


def swap(size, bit):
    return [(i, i ^ bit) for i in range(size)]


def from_next_z(block):
    up = [(2 * z, 2 * ((z + 1) % 8)) for z in range(8)]
    down = [(2 * z + 1, 2 * ((z - 1) % 8) + 1) for z in range(8)]
    return lax.ppermute(block, ("zh", "zl", "c"), up + down)


def other_core(block):
    return lax.ppermute(block, "c", swap(2, 1))


def rows_dot(left, right):
    return lax.dot_general(left, right, (((1,), (1,)), ((), ())), preferred_element_type=f32)


def in_lanes(first, total, rest):
    high = total.astype(bf16).astype(f32)
    middle = (total - high).astype(bf16).astype(f32)
    lane = lax.broadcasted_iota(jnp.int32, rest.shape, 1) - first
    low = jnp.where(lane == 2, total - high - middle, rest)
    return jnp.where(lane == 0, high, jnp.where(lane == 1, middle, low))


def local(kernel, out_shape, in_spaces, flops):
    spaces = [pl.BlockSpec(memory_space=space) for space in in_spaces]
    return pl.pallas_call(
        kernel,
        out_shape=out_shape,
        in_specs=spaces,
        out_specs=jax.tree.map(lambda _: pl.BlockSpec(memory_space=pltpu.VMEM), out_shape),
        compiler_params=pltpu.CompilerParams(vmem_limit_bytes=32 * 1024 * 1024),
        cost_estimate=pl.CostEstimate(flops=flops, bytes_accessed=3_000_000, transcendentals=0),
    )


def start_kernel(momentum_ref, raw_ref, copies_ref):
    momentum = momentum_ref[...]
    lifted = momentum * lift
    raw_ref[...] = lifted.astype(bf16)
    total = jnp.sum(momentum * momentum, keepdims=True)
    more = in_lanes(0, jnp.broadcast_to(total, (56, 128)), jnp.zeros((56, 128), f32))
    longer = jnp.concatenate([lifted, more], axis=1).astype(bf16)
    for x in range(4):
        copies_ref[x] = longer


def copies_kernel(block_ref, copies_ref):
    for x in range(4):
        copies_ref[x] = block_ref[...]


def pack(block, total):
    high = block[:, 128:]
    rest = high[88:]
    if total is None:
        spare = jnp.zeros((16, 32), f32)
    else:
        spare = in_lanes(0, jnp.broadcast_to(total, (16, 32)), jnp.zeros((16, 32), f32))
    beside = jnp.concatenate([rest[:, :32], rest[:, 32:64], rest[:, 64:], spare], axis=0)
    below = jnp.concatenate([high[:88], beside], axis=1)
    return jnp.concatenate([block[:, :128], below], axis=0)


def unpack(packed):
    beside = packed[112:, 96:]
    rest = jnp.concatenate([beside[:24], beside[24:48], beside[48:72]], axis=1)
    high = jnp.concatenate([packed[112:, :96], rest], axis=0)
    return jnp.concatenate([packed[:112], high], axis=1)


def packed_total(packed):
    return jnp.sum(packed[184:192, 96:][:1], axis=1, keepdims=True)


def parts_kernel(place_ref, totals_ref, part_a_ref, part_b_ref, part_c_ref, rows_ref, rows_x_ref, parts_ref):
    zl, first = place_ref[0], place_ref[1] == 0
    part_d = lax.dot_general(
        rows_ref[...], rows_x_ref[...], (((1,), (1,)), ((), ())), preferred_element_type=f32
    )
    total = jnp.zeros((8, 128), f32)
    for x in range(4):
        total += totals_ref[x].astype(f32)
    total = jnp.sum(total[:1], axis=1, keepdims=True)
    for own, other, l in ((part_a_ref, part_c_ref, zl), (part_b_ref, part_d, 1 - zl)):
        for zh in range(4):
            mine, its = own[56 * zh : 56 * zh + 56, :], other[56 * zh : 56 * zh + 56, :]
            block = jnp.concatenate(
                [jnp.where(first, mine, its), jnp.where(first, its, mine)], axis=0
            )
            parts_ref[2 * zh + l] = pack(block, total).astype(bf16)


def add_shares_kernel(shares_ref, piece_ref, copies_ref):
    summed = shares_ref[0].astype(f32)
    for share in range(1, 8):
        summed += shares_ref[share].astype(f32)
    row = lax.broadcasted_iota(jnp.int32, (200, 128), 0)
    with_total = in_lanes(96, packed_total(summed), summed)
    piece = jnp.where(row >= 184, with_total, summed).astype(bf16)
    piece_ref[...] = piece
    for share in range(8):
        copies_ref[share] = piece


def polynomial_kernel(left_ref, right_ref, gram_ref, poly_ref, factor_ref):
    square = jnp.zeros((112, 224), f32)
    total = jnp.zeros((1, 1), f32)
    for z in range(8):
        rights = [unpack(right_ref[x, z].astype(f32)) for x in range(4)]
        for c in range(2):
            left = left_ref[2 * z + c].astype(f32)
            total += packed_total(left)
            right = jnp.concatenate([block[56 * c : 56 * c + 56] for block in rights], axis=0)
            square += jnp.dot(
                unpack(left).astype(bf16), right.astype(bf16), preferred_element_type=f32
            )
    factor = math.sqrt(M) / 3.0 / (jnp.sqrt(total) + 1e-07)
    factor2 = (factor / lift) * (factor / lift)
    gram = (unpack(gram_ref[...].astype(f32)) * factor2).astype(bf16).astype(f32)
    square = ((square * factor2) * factor2).astype(bf16).astype(f32)
    poly = pack(coef_b * gram + coef_c * square, None).astype(bf16)
    for share in range(8):
        poly_ref[share] = poly
    factor_ref[...] = jnp.broadcast_to(factor, (8, 128))


def product_kernel(place_ref, poly_ref, rows_a_ref, rows_b_ref, rows_c_ref, rows_d_ref, product_ref, diagonal_ref):
    zl, first = place_ref[0], place_ref[1] == 0
    product = None
    for own, other, l in ((rows_a_ref, rows_c_ref, zl), (rows_b_ref, rows_d_ref, 1 - zl)):
        blocks = [unpack(poly_ref[2 * zh + l].astype(f32)) for zh in range(4)]
        lower = jnp.concatenate([block[:56] for block in blocks], axis=0)
        upper = jnp.concatenate([block[56:] for block in blocks], axis=0)
        for rows, poly in (
            (own, jnp.where(first, lower, upper)),
            (other, jnp.where(first, upper, lower)),
        ):
            term = lax.dot_general(
                poly.astype(bf16), rows[...], (((0,), (0,)), ((), ())), preferred_element_type=f32
            )
            product = term if product is None else product + term
    for x in range(4):
        product_ref[x] = product[56 * x : 56 * x + 56].astype(bf16)
    block = unpack(poly_ref[2 * place_ref[2] + zl].astype(f32))
    block = jnp.where(first, block[:56], block[56:])
    row = lax.broadcasted_iota(jnp.int32, (56, 224), 0)
    lane = lax.broadcasted_iota(jnp.int32, (56, 224), 1)
    diagonal = jnp.where(lane == row + 56 * place_ref[3], block, 0.0)
    diagonal_ref[...] = jnp.broadcast_to(jnp.sum(diagonal, axis=1, keepdims=True), (56, 128))


def update_kernel(momentum_ref, product_ref, diagonal_ref, factor_ref, update_ref):
    factor = factor_ref[:1, :1]
    product = product_ref[0].astype(f32)
    for x in range(1, 4):
        product += product_ref[x].astype(f32)
    momentum = momentum_ref[...]
    iterate = (momentum * factor).astype(bf16).astype(f32)
    small = factor / lift
    change = iterate - small * (momentum * lift).astype(bf16).astype(f32)
    product = small * product + diagonal_ref[:, :1] * change
    update_ref[...] = ((coef_a * iterate + product) * (0.2 * math.sqrt(N))).astype(bf16)


def per_device(momentum):
    place = jnp.stack([lax.axis_index(name) for name in ("zl", "c", "zh", "x")]).astype(jnp.int32)
    short, copies = local(
        start_kernel,
        [jax.ShapeDtypeStruct((56, 1664), bf16), jax.ShapeDtypeStruct((4, 56, 1792), bf16)],
        [pltpu.VMEM],
        1_000_000,
    )(momentum)

    rows_a = lax.all_gather(short, "zh", axis=0, tiled=True)
    rows_a, copies = lax.optimization_barrier((rows_a, copies))
    gathered_x = lax.all_to_all(copies, "x", 0, 0)
    rows_x = gathered_x[:, :, :1664].reshape(224, 1664)
    rows_b = from_next_z(rows_a)
    rows_c = other_core(rows_a)
    rows_d = other_core(rows_b)

    parts = local(
        parts_kernel,
        jax.ShapeDtypeStruct((8, 200, 128), bf16),
        [pltpu.SMEM] + [pltpu.VMEM] * 6,
        2 * 224 * 224 * 1664,
    )(
        place,
        gathered_x[:, :8, 1664:],
        *(rows_dot(rows, rows_x) for rows in (rows_a, rows_b, rows_c)),
        rows_d,
        rows_x,
    )
    piece, copies = local(
        add_shares_kernel,
        [jax.ShapeDtypeStruct((200, 128), bf16), jax.ShapeDtypeStruct((8, 200, 128), bf16)],
        [pltpu.VMEM],
        1_000_000,
    )(lax.all_to_all(parts, "y", 0, 0))

    right = lax.all_to_all(copies, "y", 0, 0)
    right, piece = lax.optimization_barrier((right, piece))
    copies = local(
        copies_kernel, jax.ShapeDtypeStruct((4, 8, 200, 128), bf16), [pltpu.VMEM], 1_000_000
    )(right)
    right = lax.all_to_all(copies, "x", 0, 0)
    left = lax.all_gather(piece, ("zh", "zl", "c"), axis=0)
    poly, factor = local(
        polynomial_kernel,
        [jax.ShapeDtypeStruct((8, 200, 128), bf16), jax.ShapeDtypeStruct((8, 128), f32)],
        [pltpu.VMEM] * 3,
        2 * 112 * 224 * M,
    )(left, right, piece)

    poly = lax.all_to_all(poly, "y", 0, 0)
    product, diagonal = local(
        product_kernel,
        [jax.ShapeDtypeStruct((4, 56, 1664), bf16), jax.ShapeDtypeStruct((56, 128), f32)],
        [pltpu.SMEM] + [pltpu.VMEM] * 5,
        2 * 896 * 224 * 1664,
    )(place, poly, rows_a, rows_b, rows_c, rows_d)
    return local(
        update_kernel,
        jax.ShapeDtypeStruct((56, 1664), bf16),
        [pltpu.VMEM] * 4,
        1_000_000,
    )(momentum, lax.all_to_all(product, "x", 0, 0), diagonal, factor)


def solution(mesh):
    names = ("x", "zh", "zl", "c", "y")
    fine = Mesh(mesh.devices.reshape(4, 4, 2, 2, 8), names)
    spec = P(names[:4], "y")
    return jax.shard_map(
        per_device, mesh=fine, in_specs=(spec,), out_specs=spec, check_vma=False
    )
```

```python
import math

import jax
import jax.numpy as jnp
from jax import lax
from jax.experimental import pallas as pl
from jax.experimental.pallas import tpu as pltpu
from jax.sharding import Mesh, PartitionSpec as P

M = 3584
N = 13312

coef_a = 3.4445
coef_b = -4.775
coef_c = 2.0315

lift = 2.0**14

bf16 = jnp.bfloat16
f32 = jnp.float32


def swap(size, bit):
    return [(i, i ^ bit) for i in range(size)]


def from_next_z(block):
    up = [(2 * z, 2 * ((z + 1) % 8)) for z in range(8)]
    down = [(2 * z + 1, 2 * ((z - 1) % 8) + 1) for z in range(8)]
    return lax.ppermute(block, ("zh", "zl", "c"), up + down)


def other_core(block):
    return lax.ppermute(block, "c", swap(2, 1))


def rows_dot(left, right):
    return lax.dot_general(left, right, (((1,), (1,)), ((), ())), preferred_element_type=f32)


def in_lanes(first, total, rest):
    high = total.astype(bf16).astype(f32)
    middle = (total - high).astype(bf16).astype(f32)
    lane = lax.broadcasted_iota(jnp.int32, rest.shape, 1) - first
    low = jnp.where(lane == 2, total - high - middle, rest)
    return jnp.where(lane == 0, high, jnp.where(lane == 1, middle, low))


def local(kernel, out_shape, in_spaces, flops):
    spaces = [pl.BlockSpec(memory_space=space) for space in in_spaces]
    return pl.pallas_call(
        kernel,
        out_shape=out_shape,
        in_specs=spaces,
        out_specs=jax.tree.map(lambda _: pl.BlockSpec(memory_space=pltpu.VMEM), out_shape),
        compiler_params=pltpu.CompilerParams(vmem_limit_bytes=32 * 1024 * 1024),
        cost_estimate=pl.CostEstimate(flops=flops, bytes_accessed=3_000_000, transcendentals=0),
    )


def start_kernel(momentum_ref, raw_ref, copies_ref):
    momentum = momentum_ref[...]
    lifted = momentum * lift
    raw_ref[...] = lifted.astype(bf16)
    total = jnp.sum(momentum * momentum, keepdims=True)
    more = in_lanes(0, jnp.broadcast_to(total, (56, 128)), jnp.zeros((56, 128), f32))
    longer = jnp.concatenate([lifted, more], axis=1).astype(bf16)
    for x in range(4):
        copies_ref[x] = longer


def pack(block, total):
    high = block[:, 128:]
    rest = high[88:]
    if total is None:
        spare = jnp.zeros((16, 32), f32)
    else:
        spare = in_lanes(0, jnp.broadcast_to(total, (16, 32)), jnp.zeros((16, 32), f32))
    beside = jnp.concatenate([rest[:, :32], rest[:, 32:64], rest[:, 64:], spare], axis=0)
    below = jnp.concatenate([high[:88], beside], axis=1)
    return jnp.concatenate([block[:, :128], below], axis=0)


def unpack(packed):
    beside = packed[112:, 96:]
    rest = jnp.concatenate([beside[:24], beside[24:48], beside[48:72]], axis=1)
    high = jnp.concatenate([packed[112:, :96], rest], axis=0)
    return jnp.concatenate([packed[:112], high], axis=1)


def packed_total(packed):
    return jnp.sum(packed[184:192, 96:][:1], axis=1, keepdims=True)


def parts_kernel(place_ref, totals_ref, part_a_ref, part_b_ref, part_c_ref, rows_ref, rows_x_ref, parts_ref):
    zl, first = place_ref[0], place_ref[1] == 0
    part_d = lax.dot_general(
        rows_ref[...], rows_x_ref[...], (((1,), (1,)), ((), ())), preferred_element_type=f32
    )
    total = jnp.zeros((8, 128), f32)
    for x in range(4):
        total += totals_ref[x].astype(f32)
    total = jnp.sum(total[:1], axis=1, keepdims=True)
    for own, other, l in ((part_a_ref, part_c_ref, zl), (part_b_ref, part_d, 1 - zl)):
        for zh in range(4):
            mine, its = own[56 * zh : 56 * zh + 56, :], other[56 * zh : 56 * zh + 56, :]
            block = jnp.concatenate(
                [jnp.where(first, mine, its), jnp.where(first, its, mine)], axis=0
            )
            parts_ref[2 * zh + l] = pack(block, total).astype(bf16)


def add_shares_kernel(shares_ref, piece_ref, copies_ref):
    summed = shares_ref[0].astype(f32)
    for share in range(1, 8):
        summed += shares_ref[share].astype(f32)
    row = lax.broadcasted_iota(jnp.int32, (200, 128), 0)
    with_total = in_lanes(96, packed_total(summed), summed)
    piece = jnp.where(row >= 184, with_total, summed).astype(bf16)
    piece_ref[...] = piece
    for share in range(8):
        copies_ref[share] = piece


def polynomial_kernel(left_ref, right_ref, gram_ref, poly_ref, factor_ref):
    square = jnp.zeros((112, 224), f32)
    total = jnp.zeros((1, 1), f32)
    for z in range(8):
        rights = [unpack(right_ref[x, z].astype(f32)) for x in range(4)]
        for c in range(2):
            left = left_ref[2 * z + c].astype(f32)
            total += packed_total(left)
            right = jnp.concatenate([block[56 * c : 56 * c + 56] for block in rights], axis=0)
            square += jnp.dot(
                unpack(left).astype(bf16), right.astype(bf16), preferred_element_type=f32
            )
    factor = math.sqrt(M) / 3.0 / (jnp.sqrt(total) + 1e-07)
    factor2 = (factor / lift) * (factor / lift)
    gram = (unpack(gram_ref[...].astype(f32)) * factor2).astype(bf16).astype(f32)
    square = ((square * factor2) * factor2).astype(bf16).astype(f32)
    poly = pack(coef_b * gram + coef_c * square, None).astype(bf16)
    for share in range(8):
        poly_ref[share] = poly
    factor_ref[...] = jnp.broadcast_to(factor, (8, 128))


def product_kernel(place_ref, poly_ref, rows_a_ref, rows_b_ref, rows_c_ref, rows_d_ref, product_ref, diagonal_ref):
    zl, first = place_ref[0], place_ref[1] == 0
    product = None
    for own, other, l in ((rows_a_ref, rows_c_ref, zl), (rows_b_ref, rows_d_ref, 1 - zl)):
        blocks = [unpack(poly_ref[2 * zh + l].astype(f32)) for zh in range(4)]
        lower = jnp.concatenate([block[:56] for block in blocks], axis=0)
        upper = jnp.concatenate([block[56:] for block in blocks], axis=0)
        for rows, poly in (
            (own, jnp.where(first, lower, upper)),
            (other, jnp.where(first, upper, lower)),
        ):
            term = lax.dot_general(
                poly.astype(bf16), rows[...], (((0,), (0,)), ((), ())), preferred_element_type=f32
            )
            product = term if product is None else product + term
    for x in range(4):
        product_ref[x] = product[56 * x : 56 * x + 56].astype(bf16)
    block = unpack(poly_ref[2 * place_ref[2] + zl].astype(f32))
    block = jnp.where(first, block[:56], block[56:])
    row = lax.broadcasted_iota(jnp.int32, (56, 224), 0)
    lane = lax.broadcasted_iota(jnp.int32, (56, 224), 1)
    diagonal = jnp.where(lane == row + 56 * place_ref[3], block, 0.0)
    diagonal_ref[...] = jnp.broadcast_to(jnp.sum(diagonal, axis=1, keepdims=True), (56, 128))


def update_kernel(momentum_ref, product_ref, diagonal_ref, factor_ref, update_ref):
    factor = factor_ref[:1, :1]
    product = product_ref[0].astype(f32)
    for x in range(1, 4):
        product += product_ref[x].astype(f32)
    momentum = momentum_ref[...]
    iterate = (momentum * factor).astype(bf16).astype(f32)
    small = factor / lift
    change = iterate - small * (momentum * lift).astype(bf16).astype(f32)
    product = small * product + diagonal_ref[:, :1] * change
    update_ref[...] = ((coef_a * iterate + product) * (0.2 * math.sqrt(N))).astype(bf16)


def per_device(momentum):
    place = jnp.stack([lax.axis_index(name) for name in ("zl", "c", "zh", "x")]).astype(jnp.int32)
    short, copies = local(
        start_kernel,
        [jax.ShapeDtypeStruct((56, 1664), bf16), jax.ShapeDtypeStruct((4, 56, 1792), bf16)],
        [pltpu.VMEM],
        1_000_000,
    )(momentum)

    rows_a = lax.all_gather(short, "zh", axis=0, tiled=True)
    rows_a, copies = lax.optimization_barrier((rows_a, copies))
    gathered_x = lax.all_to_all(copies, "x", 0, 0)
    rows_x = gathered_x[:, :, :1664].reshape(224, 1664)
    rows_b = from_next_z(rows_a)
    rows_c = other_core(rows_a)
    rows_d = other_core(rows_b)

    parts = local(
        parts_kernel,
        jax.ShapeDtypeStruct((8, 200, 128), bf16),
        [pltpu.SMEM] + [pltpu.VMEM] * 6,
        2 * 224 * 224 * 1664,
    )(
        place,
        gathered_x[:, :8, 1664:],
        *(rows_dot(rows, rows_x) for rows in (rows_a, rows_b, rows_c)),
        rows_d,
        rows_x,
    )
    piece, copies = local(
        add_shares_kernel,
        [jax.ShapeDtypeStruct((200, 128), bf16), jax.ShapeDtypeStruct((8, 200, 128), bf16)],
        [pltpu.VMEM],
        1_000_000,
    )(lax.all_to_all(parts, "y", 0, 0))

    right = lax.all_to_all(copies, "y", 0, 0)
    right, piece = lax.optimization_barrier((right, piece))
    copies = jnp.broadcast_to(right[None], (4, *right.shape))
    right = lax.all_to_all(copies, "x", 0, 0)
    left = lax.all_gather(piece, ("zh", "zl", "c"), axis=0)
    poly, factor = local(
        polynomial_kernel,
        [jax.ShapeDtypeStruct((8, 200, 128), bf16), jax.ShapeDtypeStruct((8, 128), f32)],
        [pltpu.VMEM] * 3,
        2 * 112 * 224 * M,
    )(left, right, piece)

    poly = lax.all_to_all(poly, "y", 0, 0)
    product, diagonal = local(
        product_kernel,
        [jax.ShapeDtypeStruct((4, 56, 1664), bf16), jax.ShapeDtypeStruct((56, 128), f32)],
        [pltpu.SMEM] + [pltpu.VMEM] * 5,
        2 * 896 * 224 * 1664,
    )(place, poly, rows_a, rows_b, rows_c, rows_d)
    return local(
        update_kernel,
        jax.ShapeDtypeStruct((56, 1664), bf16),
        [pltpu.VMEM] * 4,
        1_000_000,
    )(momentum, lax.all_to_all(product, "x", 0, 0), diagonal, factor)


def solution(mesh):
    names = ("x", "zh", "zl", "c", "y")
    fine = Mesh(mesh.devices.reshape(4, 4, 2, 2, 8), names)
    spec = P(names[:4], "y")
    return jax.shard_map(
        per_device, mesh=fine, in_specs=(spec,), out_specs=spec, check_vma=False
    )
```

```python
import math

import jax
import jax.numpy as jnp
from jax import lax
from jax.experimental import pallas as pl
from jax.experimental.pallas import tpu as pltpu
from jax.sharding import Mesh, PartitionSpec as P

M = 3584
N = 13312

coef_a = 3.4445
coef_b = -4.775
coef_c = 2.0315

lift = 2.0**14

bf16 = jnp.bfloat16
f32 = jnp.float32


def swap(size, bit):
    return [(i, i ^ bit) for i in range(size)]


def from_next_z(block):
    up = [(2 * z, 2 * ((z + 1) % 8)) for z in range(8)]
    down = [(2 * z + 1, 2 * ((z - 1) % 8) + 1) for z in range(8)]
    return lax.ppermute(block, ("zh", "zl", "c"), up + down)


def other_core(block):
    return lax.ppermute(block, "c", swap(2, 1))


def rows_dot(left, right):
    return lax.dot_general(left, right, (((1,), (1,)), ((), ())), preferred_element_type=f32)


def in_lanes(first, total, rest):
    high = total.astype(bf16).astype(f32)
    middle = (total - high).astype(bf16).astype(f32)
    lane = lax.broadcasted_iota(jnp.int32, rest.shape, 1) - first
    low = jnp.where(lane == 2, total - high - middle, rest)
    return jnp.where(lane == 0, high, jnp.where(lane == 1, middle, low))


def local(kernel, out_shape, in_spaces, flops):
    spaces = [pl.BlockSpec(memory_space=space) for space in in_spaces]
    return pl.pallas_call(
        kernel,
        out_shape=out_shape,
        in_specs=spaces,
        out_specs=jax.tree.map(lambda _: pl.BlockSpec(memory_space=pltpu.VMEM), out_shape),
        compiler_params=pltpu.CompilerParams(vmem_limit_bytes=32 * 1024 * 1024),
        cost_estimate=pl.CostEstimate(flops=flops, bytes_accessed=3_000_000, transcendentals=0),
    )


def start_kernel(momentum_ref, raw_ref, copies_ref):
    momentum = momentum_ref[...]
    lifted = momentum * lift
    raw_ref[...] = lifted.astype(bf16)
    total = jnp.sum(momentum * momentum, keepdims=True)
    more = in_lanes(0, jnp.broadcast_to(total, (56, 128)), jnp.zeros((56, 128), f32))
    longer = jnp.concatenate([lifted, more], axis=1).astype(bf16)
    for x in range(4):
        copies_ref[x] = longer


def pack(block, total):
    high = block[:, 128:]
    rest = high[88:]
    if total is None:
        spare = jnp.zeros((16, 32), f32)
    else:
        spare = in_lanes(0, jnp.broadcast_to(total, (16, 32)), jnp.zeros((16, 32), f32))
    beside = jnp.concatenate([rest[:, :32], rest[:, 32:64], rest[:, 64:], spare], axis=0)
    below = jnp.concatenate([high[:88], beside], axis=1)
    return jnp.concatenate([block[:, :128], below], axis=0)


def unpack(packed):
    beside = packed[112:, 96:]
    rest = jnp.concatenate([beside[:24], beside[24:48], beside[48:72]], axis=1)
    high = jnp.concatenate([packed[112:, :96], rest], axis=0)
    return jnp.concatenate([packed[:112], high], axis=1)


def packed_total(packed):
    return jnp.sum(packed[184:192, 96:][:1], axis=1, keepdims=True)


def with_other(first, own, other, zh, total):
    mine, its = own[56 * zh : 56 * zh + 56, :], other[56 * zh : 56 * zh + 56, :]
    block = jnp.concatenate([jnp.where(first, mine, its), jnp.where(first, its, mine)], axis=0)
    return pack(block, total).astype(bf16)


def same_kernel(place_ref, totals_ref, part_a_ref, part_c_ref, same_ref, total_ref):
    total = jnp.zeros((8, 128), f32)
    for x in range(4):
        total += totals_ref[x].astype(f32)
    total = jnp.sum(total[:1], axis=1, keepdims=True)
    total_ref[...] = jnp.broadcast_to(total, (8, 128))
    for zh in range(4):
        same_ref[zh] = with_other(place_ref[1] == 0, part_a_ref, part_c_ref, zh, total)


def parts_kernel(place_ref, total_ref, same_ref, part_b_ref, rows_ref, rows_x_ref, parts_ref):
    zl = place_ref[0]
    part_d = lax.dot_general(
        rows_ref[...], rows_x_ref[...], (((1,), (1,)), ((), ())), preferred_element_type=f32
    )
    total = total_ref[:1, :1]
    for zh in range(4):
        parts_ref[2 * zh + zl] = same_ref[zh]
        parts_ref[2 * zh + 1 - zl] = with_other(place_ref[1] == 0, part_b_ref, part_d, zh, total)


def add_shares_kernel(shares_ref, piece_ref, copies_ref):
    summed = shares_ref[0].astype(f32)
    for share in range(1, 8):
        summed += shares_ref[share].astype(f32)
    row = lax.broadcasted_iota(jnp.int32, (200, 128), 0)
    with_total = in_lanes(96, packed_total(summed), summed)
    piece = jnp.where(row >= 184, with_total, summed).astype(bf16)
    piece_ref[...] = piece
    for share in range(8):
        copies_ref[share] = piece


def polynomial_kernel(left_ref, right_ref, gram_ref, poly_ref, factor_ref):
    square = jnp.zeros((112, 224), f32)
    total = jnp.zeros((1, 1), f32)
    for z in range(8):
        rights = [unpack(right_ref[x, z].astype(f32)) for x in range(4)]
        for c in range(2):
            left = left_ref[2 * z + c].astype(f32)
            total += packed_total(left)
            right = jnp.concatenate([block[56 * c : 56 * c + 56] for block in rights], axis=0)
            square += jnp.dot(
                unpack(left).astype(bf16), right.astype(bf16), preferred_element_type=f32
            )
    factor = math.sqrt(M) / 3.0 / (jnp.sqrt(total) + 1e-07)
    factor2 = (factor / lift) * (factor / lift)
    gram = (unpack(gram_ref[...].astype(f32)) * factor2).astype(bf16).astype(f32)
    square = ((square * factor2) * factor2).astype(bf16).astype(f32)
    poly = pack(coef_b * gram + coef_c * square, None).astype(bf16)
    for share in range(8):
        poly_ref[share] = poly
    factor_ref[...] = jnp.broadcast_to(factor, (8, 128))


def product_kernel(place_ref, poly_ref, rows_a_ref, rows_b_ref, rows_c_ref, rows_d_ref, product_ref, diagonal_ref):
    zl, first = place_ref[0], place_ref[1] == 0
    product = None
    for own, other, l in ((rows_a_ref, rows_c_ref, zl), (rows_b_ref, rows_d_ref, 1 - zl)):
        blocks = [unpack(poly_ref[2 * zh + l].astype(f32)) for zh in range(4)]
        lower = jnp.concatenate([block[:56] for block in blocks], axis=0)
        upper = jnp.concatenate([block[56:] for block in blocks], axis=0)
        for rows, poly in (
            (own, jnp.where(first, lower, upper)),
            (other, jnp.where(first, upper, lower)),
        ):
            term = lax.dot_general(
                poly.astype(bf16), rows[...], (((0,), (0,)), ((), ())), preferred_element_type=f32
            )
            product = term if product is None else product + term
    for x in range(4):
        product_ref[x] = product[56 * x : 56 * x + 56].astype(bf16)
    block = unpack(poly_ref[2 * place_ref[2] + zl].astype(f32))
    block = jnp.where(first, block[:56], block[56:])
    row = lax.broadcasted_iota(jnp.int32, (56, 224), 0)
    lane = lax.broadcasted_iota(jnp.int32, (56, 224), 1)
    diagonal = jnp.where(lane == row + 56 * place_ref[3], block, 0.0)
    diagonal_ref[...] = jnp.broadcast_to(jnp.sum(diagonal, axis=1, keepdims=True), (56, 128))


def update_kernel(momentum_ref, product_ref, diagonal_ref, factor_ref, update_ref):
    factor = factor_ref[:1, :1]
    product = product_ref[0].astype(f32)
    for x in range(1, 4):
        product += product_ref[x].astype(f32)
    momentum = momentum_ref[...]
    iterate = (momentum * factor).astype(bf16).astype(f32)
    small = factor / lift
    change = iterate - small * (momentum * lift).astype(bf16).astype(f32)
    product = small * product + diagonal_ref[:, :1] * change
    update_ref[...] = ((coef_a * iterate + product) * (0.2 * math.sqrt(N))).astype(bf16)


def per_device(momentum):
    place = jnp.stack([lax.axis_index(name) for name in ("zl", "c", "zh", "x")]).astype(jnp.int32)
    short, copies = local(
        start_kernel,
        [jax.ShapeDtypeStruct((56, 1664), bf16), jax.ShapeDtypeStruct((4, 56, 1792), bf16)],
        [pltpu.VMEM],
        1_000_000,
    )(momentum)

    rows_a = lax.all_gather(short, "zh", axis=0, tiled=True)
    rows_a, copies = lax.optimization_barrier((rows_a, copies))
    gathered_x = lax.all_to_all(copies, "x", 0, 0)
    rows_x = gathered_x[:, :, :1664].reshape(224, 1664)
    rows_b = from_next_z(rows_a)
    rows_c = other_core(rows_a)
    rows_d = other_core(rows_b)

    same, total = local(
        same_kernel,
        [jax.ShapeDtypeStruct((4, 200, 128), bf16), jax.ShapeDtypeStruct((8, 128), f32)],
        [pltpu.SMEM] + [pltpu.VMEM] * 3,
        1_000_000,
    )(place, gathered_x[:, :8, 1664:], rows_dot(rows_a, rows_x), rows_dot(rows_c, rows_x))
    parts = local(
        parts_kernel,
        jax.ShapeDtypeStruct((8, 200, 128), bf16),
        [pltpu.SMEM] + [pltpu.VMEM] * 5,
        2 * 224 * 224 * 1664,
    )(place, total, same, rows_dot(rows_b, rows_x), rows_d, rows_x)
    piece, copies = local(
        add_shares_kernel,
        [jax.ShapeDtypeStruct((200, 128), bf16), jax.ShapeDtypeStruct((8, 200, 128), bf16)],
        [pltpu.VMEM],
        1_000_000,
    )(lax.all_to_all(parts, "y", 0, 0))

    right = lax.all_to_all(copies, "y", 0, 0)
    right, piece = lax.optimization_barrier((right, piece))
    copies = jnp.broadcast_to(right[None], (4, *right.shape))
    right = lax.all_to_all(copies, "x", 0, 0)
    left = lax.all_gather(piece, ("zh", "zl", "c"), axis=0)
    poly, factor = local(
        polynomial_kernel,
        [jax.ShapeDtypeStruct((8, 200, 128), bf16), jax.ShapeDtypeStruct((8, 128), f32)],
        [pltpu.VMEM] * 3,
        2 * 112 * 224 * M,
    )(left, right, piece)

    poly = lax.all_to_all(poly, "y", 0, 0)
    product, diagonal = local(
        product_kernel,
        [jax.ShapeDtypeStruct((4, 56, 1664), bf16), jax.ShapeDtypeStruct((56, 128), f32)],
        [pltpu.SMEM] + [pltpu.VMEM] * 5,
        2 * 896 * 224 * 1664,
    )(place, poly, rows_a, rows_b, rows_c, rows_d)
    return local(
        update_kernel,
        jax.ShapeDtypeStruct((56, 1664), bf16),
        [pltpu.VMEM] * 4,
        1_000_000,
    )(momentum, lax.all_to_all(product, "x", 0, 0), diagonal, factor)


def solution(mesh):
    names = ("x", "zh", "zl", "c", "y")
    fine = Mesh(mesh.devices.reshape(4, 4, 2, 2, 8), names)
    spec = P(names[:4], "y")
    return jax.shard_map(
        per_device, mesh=fine, in_specs=(spec,), out_specs=spec, check_vma=False
    )
```

```python
import math

import jax
import jax.numpy as jnp
from jax import lax
from jax.experimental import pallas as pl
from jax.experimental.pallas import tpu as pltpu
from jax.sharding import Mesh, PartitionSpec as P

M = 3584
N = 13312

coef_a = 3.4445
coef_b = -4.775
coef_c = 2.0315

lift = 2.0**14

bf16 = jnp.bfloat16
f32 = jnp.float32


def swap(size, bit):
    return [(i, i ^ bit) for i in range(size)]


def from_next_z(block):
    up = [(2 * z, 2 * ((z + 1) % 8)) for z in range(8)]
    down = [(2 * z + 1, 2 * ((z - 1) % 8) + 1) for z in range(8)]
    return lax.ppermute(block, ("zh", "zl", "c"), up + down)


def other_core(block):
    return lax.ppermute(block, "c", swap(2, 1))


def rows_dot(left, right):
    return lax.dot_general(left, right, (((1,), (1,)), ((), ())), preferred_element_type=f32)


def in_lanes(first, total, rest):
    high = total.astype(bf16).astype(f32)
    middle = (total - high).astype(bf16).astype(f32)
    lane = lax.broadcasted_iota(jnp.int32, rest.shape, 1) - first
    low = jnp.where(lane == 2, total - high - middle, rest)
    return jnp.where(lane == 0, high, jnp.where(lane == 1, middle, low))


def local(kernel, out_shape, in_spaces, flops):
    spaces = [pl.BlockSpec(memory_space=space) for space in in_spaces]
    return pl.pallas_call(
        kernel,
        out_shape=out_shape,
        in_specs=spaces,
        out_specs=jax.tree.map(lambda _: pl.BlockSpec(memory_space=pltpu.VMEM), out_shape),
        compiler_params=pltpu.CompilerParams(vmem_limit_bytes=32 * 1024 * 1024),
        cost_estimate=pl.CostEstimate(flops=flops, bytes_accessed=3_000_000, transcendentals=0),
    )


def start_kernel(momentum_ref, raw_ref, copies_ref):
    momentum = momentum_ref[...]
    lifted = momentum * lift
    raw_ref[...] = lifted.astype(bf16)
    total = jnp.sum(momentum * momentum, keepdims=True)
    more = in_lanes(0, jnp.broadcast_to(total, (56, 128)), jnp.zeros((56, 128), f32))
    longer = jnp.concatenate([lifted, more], axis=1).astype(bf16)
    for x in range(4):
        copies_ref[x] = longer


def pack(block, total):
    high = block[:, 128:]
    rest = high[88:]
    if total is None:
        spare = jnp.zeros((16, 32), f32)
    else:
        spare = in_lanes(0, jnp.broadcast_to(total, (16, 32)), jnp.zeros((16, 32), f32))
    beside = jnp.concatenate([rest[:, :32], rest[:, 32:64], rest[:, 64:], spare], axis=0)
    below = jnp.concatenate([high[:88], beside], axis=1)
    return jnp.concatenate([block[:, :128], below], axis=0)


def unpack(packed):
    beside = packed[112:, 96:]
    rest = jnp.concatenate([beside[:24], beside[24:48], beside[48:72]], axis=1)
    high = jnp.concatenate([packed[112:, :96], rest], axis=0)
    return jnp.concatenate([packed[:112], high], axis=1)


def packed_total(packed):
    return jnp.sum(packed[184:192, 96:][:1], axis=1, keepdims=True)


def parts_kernel(place_ref, totals_ref, part_a_ref, part_b_ref, part_c_ref, rows_ref, rows_x_ref, parts_ref):
    zl, first = place_ref[0], place_ref[1] == 0
    part_d = lax.dot_general(
        rows_ref[...], rows_x_ref[...], (((1,), (1,)), ((), ())), preferred_element_type=f32
    )
    total = jnp.zeros((8, 128), f32)
    for x in range(4):
        total += totals_ref[x].astype(f32)
    total = jnp.sum(total[:1], axis=1, keepdims=True)
    for own, other, l in ((part_a_ref, part_c_ref, zl), (part_b_ref, part_d, 1 - zl)):
        for zh in range(4):
            mine, its = own[56 * zh : 56 * zh + 56, :], other[56 * zh : 56 * zh + 56, :]
            block = jnp.concatenate(
                [jnp.where(first, mine, its), jnp.where(first, its, mine)], axis=0
            )
            parts_ref[2 * zh + l] = pack(block, total).astype(bf16)


def add_shares_kernel(shares_ref, piece_ref, copies_ref):
    summed = shares_ref[0].astype(f32)
    for share in range(1, 8):
        summed += shares_ref[share].astype(f32)
    row = lax.broadcasted_iota(jnp.int32, (200, 128), 0)
    with_total = in_lanes(96, packed_total(summed), summed)
    piece = jnp.where(row >= 184, with_total, summed).astype(bf16)
    piece_ref[...] = piece
    for share in range(8):
        copies_ref[share] = piece


def polynomial_kernel(left_ref, right_ref, gram_ref, poly_ref, factor_ref):
    square = jnp.zeros((112, 224), f32)
    total = jnp.zeros((1, 1), f32)
    for z in range(8):
        rights = [unpack(right_ref[x, z].astype(f32)) for x in range(4)]
        for c in range(2):
            left = left_ref[2 * z + c].astype(f32)
            total += packed_total(left)
            right = jnp.concatenate([block[56 * c : 56 * c + 56] for block in rights], axis=0)
            square += jnp.dot(
                unpack(left).astype(bf16), right.astype(bf16), preferred_element_type=f32
            )
    factor = math.sqrt(M) / 3.0 / (jnp.sqrt(total) + 1e-07)
    factor2 = (factor / lift) * (factor / lift)
    gram = (unpack(gram_ref[...].astype(f32)) * factor2).astype(bf16).astype(f32)
    square = ((square * factor2) * factor2).astype(bf16).astype(f32)
    poly = pack(coef_b * gram + coef_c * square, None).astype(bf16)
    for share in range(8):
        poly_ref[share] = poly
    factor_ref[...] = jnp.broadcast_to(factor, (8, 128))


def product_kernel(place_ref, poly_ref, rows_a_ref, rows_b_ref, rows_c_ref, rows_d_ref, product_ref, diagonal_ref):
    zl, first = place_ref[0], place_ref[1] == 0
    product = None
    for own, other, l in ((rows_a_ref, rows_c_ref, zl), (rows_b_ref, rows_d_ref, 1 - zl)):
        blocks = [unpack(poly_ref[2 * zh + l].astype(f32)) for zh in range(4)]
        lower = jnp.concatenate([block[:56] for block in blocks], axis=0)
        upper = jnp.concatenate([block[56:] for block in blocks], axis=0)
        for rows, poly in (
            (own, jnp.where(first, lower, upper)),
            (other, jnp.where(first, upper, lower)),
        ):
            term = lax.dot_general(
                poly.astype(bf16), rows[...], (((0,), (0,)), ((), ())), preferred_element_type=f32
            )
            product = term if product is None else product + term
    for x in range(4):
        product_ref[x] = product[56 * x : 56 * x + 56].astype(bf16)
    block = unpack(poly_ref[2 * place_ref[2] + zl].astype(f32))
    block = jnp.where(first, block[:56], block[56:])
    row = lax.broadcasted_iota(jnp.int32, (56, 224), 0)
    lane = lax.broadcasted_iota(jnp.int32, (56, 224), 1)
    diagonal = jnp.where(lane == row + 56 * place_ref[3], block, 0.0)
    diagonal_ref[...] = jnp.broadcast_to(jnp.sum(diagonal, axis=1, keepdims=True), (56, 128))


def update_kernel(momentum_ref, product_ref, diagonal_ref, factor_ref, update_ref):
    factor = factor_ref[:1, :1]
    product = product_ref[0].astype(f32)
    for x in range(1, 4):
        product += product_ref[x].astype(f32)
    momentum = momentum_ref[...]
    iterate = (momentum * factor).astype(bf16).astype(f32)
    small = factor / lift
    change = iterate - small * (momentum * lift).astype(bf16).astype(f32)
    product = small * product + diagonal_ref[:, :1] * change
    update_ref[...] = ((coef_a * iterate + product) * (0.2 * math.sqrt(N))).astype(bf16)


def per_device(momentum):
    place = jnp.stack([lax.axis_index(name) for name in ("zl", "c", "zh", "x")]).astype(jnp.int32)
    short, copies = local(
        start_kernel,
        [jax.ShapeDtypeStruct((56, 1664), bf16), jax.ShapeDtypeStruct((4, 56, 1792), bf16)],
        [pltpu.VMEM],
        1_000_000,
    )(momentum)

    rows_a = lax.all_gather(short, "zh", axis=0, tiled=True)
    rows_a, copies = lax.optimization_barrier((rows_a, copies))
    gathered_x = lax.all_to_all(copies, "x", 0, 0)
    rows_x = gathered_x[:, :, :1664].reshape(224, 1664)
    rows_b = from_next_z(rows_a)
    rows_c = other_core(rows_a)
    rows_d = other_core(rows_b)

    parts = local(
        parts_kernel,
        jax.ShapeDtypeStruct((8, 200, 128), bf16),
        [pltpu.SMEM] + [pltpu.VMEM] * 6,
        2 * 224 * 224 * 1664,
    )(
        place,
        gathered_x[:, :8, 1664:],
        *(rows_dot(rows, rows_x) for rows in (rows_a, rows_b, rows_c)),
        rows_d,
        rows_x,
    )
    piece, copies = local(
        add_shares_kernel,
        [jax.ShapeDtypeStruct((200, 128), bf16), jax.ShapeDtypeStruct((8, 200, 128), bf16)],
        [pltpu.VMEM],
        1_000_000,
    )(lax.all_to_all(parts, "y", 0, 0))

    right = lax.all_to_all(copies, "y", 0, 0)
    right, piece = lax.optimization_barrier((right, piece))
    copies = jnp.broadcast_to(right[None], (4, *right.shape))
    right = lax.all_to_all(copies, "x", 0, 0)
    left = lax.all_gather(piece, ("zh", "zl", "c"), axis=0, tiled=True).reshape(16, 200, 128)
    poly, factor = local(
        polynomial_kernel,
        [jax.ShapeDtypeStruct((8, 200, 128), bf16), jax.ShapeDtypeStruct((8, 128), f32)],
        [pltpu.VMEM] * 3,
        2 * 112 * 224 * M,
    )(left, right, piece)

    poly = lax.all_to_all(poly, "y", 0, 0)
    product, diagonal = local(
        product_kernel,
        [jax.ShapeDtypeStruct((4, 56, 1664), bf16), jax.ShapeDtypeStruct((56, 128), f32)],
        [pltpu.SMEM] + [pltpu.VMEM] * 5,
        2 * 896 * 224 * 1664,
    )(place, poly, rows_a, rows_b, rows_c, rows_d)
    return local(
        update_kernel,
        jax.ShapeDtypeStruct((56, 1664), bf16),
        [pltpu.VMEM] * 4,
        1_000_000,
    )(momentum, lax.all_to_all(product, "x", 0, 0), diagonal, factor)


def solution(mesh):
    names = ("x", "zh", "zl", "c", "y")
    fine = Mesh(mesh.devices.reshape(4, 4, 2, 2, 8), names)
    spec = P(names[:4], "y")
    return jax.shard_map(
        per_device, mesh=fine, in_specs=(spec,), out_specs=spec, check_vma=False
    )
```

```python
import math

import jax
import jax.numpy as jnp
from jax import lax
from jax.experimental import pallas as pl
from jax.experimental.pallas import tpu as pltpu
from jax.sharding import Mesh, PartitionSpec as P

M = 3584
N = 13312

coef_a = 3.4445
coef_b = -4.775
coef_c = 2.0315

lift = 2.0**14

bf16 = jnp.bfloat16
f32 = jnp.float32


def swap(size, bit):
    return [(i, i ^ bit) for i in range(size)]


def from_next_z(block):
    up = [(2 * z, 2 * ((z + 1) % 8)) for z in range(8)]
    down = [(2 * z + 1, 2 * ((z - 1) % 8) + 1) for z in range(8)]
    return lax.ppermute(block, ("zh", "zl", "c"), up + down)


def other_core(block):
    return lax.ppermute(block, "c", swap(2, 1))


def rows_dot(left, right):
    return lax.dot_general(left, right, (((1,), (1,)), ((), ())), preferred_element_type=f32)


def in_lanes(first, total, rest):
    high = total.astype(bf16).astype(f32)
    middle = (total - high).astype(bf16).astype(f32)
    lane = lax.broadcasted_iota(jnp.int32, rest.shape, 1) - first
    low = jnp.where(lane == 2, total - high - middle, rest)
    return jnp.where(lane == 0, high, jnp.where(lane == 1, middle, low))


def local(kernel, out_shape, in_spaces, flops):
    spaces = [pl.BlockSpec(memory_space=space) for space in in_spaces]
    return pl.pallas_call(
        kernel,
        out_shape=out_shape,
        in_specs=spaces,
        out_specs=jax.tree.map(lambda _: pl.BlockSpec(memory_space=pltpu.VMEM), out_shape),
        compiler_params=pltpu.CompilerParams(vmem_limit_bytes=32 * 1024 * 1024),
        cost_estimate=pl.CostEstimate(flops=flops, bytes_accessed=3_000_000, transcendentals=0),
    )


def start_kernel(momentum_ref, raw_ref, copies_ref):
    momentum = momentum_ref[...]
    lifted = momentum * lift
    raw_ref[...] = lifted.astype(bf16)
    total = jnp.sum(momentum * momentum, keepdims=True)
    more = in_lanes(0, jnp.broadcast_to(total, (56, 128)), jnp.zeros((56, 128), f32))
    longer = jnp.concatenate([lifted, more], axis=1).astype(bf16)
    for x in range(4):
        copies_ref[x] = longer


def pack(block, total):
    high = block[:, 128:]
    rest = high[88:]
    if total is None:
        spare = jnp.zeros((16, 32), f32)
    else:
        spare = in_lanes(0, jnp.broadcast_to(total, (16, 32)), jnp.zeros((16, 32), f32))
    beside = jnp.concatenate([rest[:, :32], rest[:, 32:64], rest[:, 64:], spare], axis=0)
    below = jnp.concatenate([high[:88], beside], axis=1)
    return jnp.concatenate([block[:, :128], below], axis=0)


def unpack(packed):
    beside = packed[112:, 96:]
    rest = jnp.concatenate([beside[:24], beside[24:48], beside[48:72]], axis=1)
    high = jnp.concatenate([packed[112:, :96], rest], axis=0)
    return jnp.concatenate([packed[:112], high], axis=1)


def packed_total(packed):
    return jnp.sum(packed[184:192, 96:][:1], axis=1, keepdims=True)


def parts_kernel(place_ref, totals_ref, part_a_ref, part_b_ref, part_c_ref, rows_ref, rows_x_ref, parts_ref):
    zl, first = place_ref[0], place_ref[1] == 0
    part_d = lax.dot_general(
        rows_ref[...], rows_x_ref[...], (((1,), (1,)), ((), ())), preferred_element_type=f32
    )
    total = jnp.zeros((8, 128), f32)
    for x in range(4):
        total += totals_ref[x].astype(f32)
    total = jnp.sum(total[:1], axis=1, keepdims=True)
    for own, other, l in ((part_a_ref, part_c_ref, zl), (part_b_ref, part_d, 1 - zl)):
        for zh in range(4):
            mine, its = own[56 * zh : 56 * zh + 56, :], other[56 * zh : 56 * zh + 56, :]
            block = jnp.concatenate(
                [jnp.where(first, mine, its), jnp.where(first, its, mine)], axis=0
            )
            parts_ref[2 * zh + l] = pack(block, total).astype(bf16)


def add_shares_kernel(shares_ref, piece_ref, copies_ref):
    summed = shares_ref[0].astype(f32)
    for share in range(1, 8):
        summed += shares_ref[share].astype(f32)
    row = lax.broadcasted_iota(jnp.int32, (200, 128), 0)
    with_total = in_lanes(96, packed_total(summed), summed)
    piece = jnp.where(row >= 184, with_total, summed).astype(bf16)
    piece_ref[...] = piece
    for share in range(8):
        copies_ref[share] = piece


def polynomial_kernel(left_ref, right_ref, gram_ref, poly_ref, factor_ref):
    square = jnp.zeros((112, 224), f32)
    total = jnp.zeros((1, 1), f32)
    for z in range(8):
        rights = [unpack(right_ref[x, z]) for x in range(4)]
        for c in range(2):
            left = left_ref[2 * z + c].astype(f32)
            total += packed_total(left)
            right = jnp.concatenate([block[56 * c : 56 * c + 56] for block in rights], axis=0)
            square += jnp.dot(
                unpack(left).astype(bf16), right, preferred_element_type=f32
            )
    factor = math.sqrt(M) / 3.0 / (jnp.sqrt(total) + 1e-07)
    factor2 = (factor / lift) * (factor / lift)
    gram = (unpack(gram_ref[...].astype(f32)) * factor2).astype(bf16).astype(f32)
    square = ((square * factor2) * factor2).astype(bf16).astype(f32)
    poly = pack(coef_b * gram + coef_c * square, None).astype(bf16)
    for share in range(8):
        poly_ref[share] = poly
    factor_ref[...] = jnp.broadcast_to(factor, (8, 128))


def product_kernel(place_ref, poly_ref, rows_a_ref, rows_b_ref, rows_c_ref, rows_d_ref, product_ref, diagonal_ref):
    zl, first = place_ref[0], place_ref[1] == 0
    product = None
    for own, other, l in ((rows_a_ref, rows_c_ref, zl), (rows_b_ref, rows_d_ref, 1 - zl)):
        blocks = [unpack(poly_ref[2 * zh + l].astype(f32)) for zh in range(4)]
        lower = jnp.concatenate([block[:56] for block in blocks], axis=0)
        upper = jnp.concatenate([block[56:] for block in blocks], axis=0)
        for rows, poly in (
            (own, jnp.where(first, lower, upper)),
            (other, jnp.where(first, upper, lower)),
        ):
            term = lax.dot_general(
                poly.astype(bf16), rows[...], (((0,), (0,)), ((), ())), preferred_element_type=f32
            )
            product = term if product is None else product + term
    for x in range(4):
        product_ref[x] = product[56 * x : 56 * x + 56].astype(bf16)
    block = unpack(poly_ref[2 * place_ref[2] + zl].astype(f32))
    block = jnp.where(first, block[:56], block[56:])
    row = lax.broadcasted_iota(jnp.int32, (56, 224), 0)
    lane = lax.broadcasted_iota(jnp.int32, (56, 224), 1)
    diagonal = jnp.where(lane == row + 56 * place_ref[3], block, 0.0)
    diagonal_ref[...] = jnp.broadcast_to(jnp.sum(diagonal, axis=1, keepdims=True), (56, 128))


def update_kernel(momentum_ref, product_ref, diagonal_ref, factor_ref, update_ref):
    factor = factor_ref[:1, :1]
    product = product_ref[0].astype(f32)
    for x in range(1, 4):
        product += product_ref[x].astype(f32)
    momentum = momentum_ref[...]
    iterate = (momentum * factor).astype(bf16).astype(f32)
    small = factor / lift
    change = iterate - small * (momentum * lift).astype(bf16).astype(f32)
    product = small * product + diagonal_ref[:, :1] * change
    update_ref[...] = ((coef_a * iterate + product) * (0.2 * math.sqrt(N))).astype(bf16)


def per_device(momentum):
    place = jnp.stack([lax.axis_index(name) for name in ("zl", "c", "zh", "x")]).astype(jnp.int32)
    short, copies = local(
        start_kernel,
        [jax.ShapeDtypeStruct((56, 1664), bf16), jax.ShapeDtypeStruct((4, 56, 1792), bf16)],
        [pltpu.VMEM],
        1_000_000,
    )(momentum)

    rows_a = lax.all_gather(short, "zh", axis=0, tiled=True)
    rows_a, copies = lax.optimization_barrier((rows_a, copies))
    gathered_x = lax.all_to_all(copies, "x", 0, 0)
    rows_x = gathered_x[:, :, :1664].reshape(224, 1664)
    rows_b = from_next_z(rows_a)
    rows_c = other_core(rows_a)
    rows_d = other_core(rows_b)

    parts = local(
        parts_kernel,
        jax.ShapeDtypeStruct((8, 200, 128), bf16),
        [pltpu.SMEM] + [pltpu.VMEM] * 6,
        2 * 224 * 224 * 1664,
    )(
        place,
        gathered_x[:, :8, 1664:],
        *(rows_dot(rows, rows_x) for rows in (rows_a, rows_b, rows_c)),
        rows_d,
        rows_x,
    )
    piece, copies = local(
        add_shares_kernel,
        [jax.ShapeDtypeStruct((200, 128), bf16), jax.ShapeDtypeStruct((8, 200, 128), bf16)],
        [pltpu.VMEM],
        1_000_000,
    )(lax.all_to_all(parts, "y", 0, 0))

    right = lax.all_to_all(copies, "y", 0, 0)
    right, piece = lax.optimization_barrier((right, piece))
    copies = jnp.broadcast_to(right[None], (4, *right.shape))
    right = lax.all_to_all(copies, "x", 0, 0)
    left = lax.all_gather(piece, ("zh", "zl", "c"), axis=0)
    poly, factor = local(
        polynomial_kernel,
        [jax.ShapeDtypeStruct((8, 200, 128), bf16), jax.ShapeDtypeStruct((8, 128), f32)],
        [pltpu.VMEM] * 3,
        2 * 112 * 224 * M,
    )(left, right, piece)

    poly = lax.all_to_all(poly, "y", 0, 0)
    product, diagonal = local(
        product_kernel,
        [jax.ShapeDtypeStruct((4, 56, 1664), bf16), jax.ShapeDtypeStruct((56, 128), f32)],
        [pltpu.SMEM] + [pltpu.VMEM] * 5,
        2 * 896 * 224 * 1664,
    )(place, poly, rows_a, rows_b, rows_c, rows_d)
    return local(
        update_kernel,
        jax.ShapeDtypeStruct((56, 1664), bf16),
        [pltpu.VMEM] * 4,
        1_000_000,
    )(momentum, lax.all_to_all(product, "x", 0, 0), diagonal, factor)


def solution(mesh):
    names = ("x", "zh", "zl", "c", "y")
    fine = Mesh(mesh.devices.reshape(4, 4, 2, 2, 8), names)
    spec = P(names[:4], "y")
    return jax.shard_map(
        per_device, mesh=fine, in_specs=(spec,), out_specs=spec, check_vma=False
    )
```
